256 devices in a mesh: tok: 32 (over y, x, core), lat: 8 (over z).
Axes of the slice: x: 4, y: 4, z: 8, core: 2. Of those that a mesh axis runs over, the one named last changes fastest.
Arguments:
- captured: bfloat16 [4096, 16384], P(None, 'tok'), may hold values from -6 to 6
- enc_weight: bfloat16 [16384, 16384], P('tok', 'lat'), may hold values from -0.046875 to 0.046875
- enc_bias: float32 [16384], P('lat'), may hold values from -3 to 3
- dec_weight: bfloat16 [16384, 16384], P('lat', 'tok'), may hold values from -0.125 to 0.125
- dec_bias: float32 [16384], P('tok'), may hold values from -1.5 to 1.5
- block_ids: int32 [32, 8, 2], P(None, 'lat'), may hold values from 0 to 15, as said below
- block_counts: int32 [32, 8], P(None, 'lat'), may hold values from 1 to 2, as said below
Outputs:
- enc_grad: bfloat16 [16384, 16384], P('tok', 'lat')
- dec_grad: bfloat16 [16384, 16384], P('lat', 'tok')
The draws below stay inside these ranges and needn't reach their ends.
Inputs may be any that keep to these rules, and one draw needn't show every extreme that they name: block_ids[b, s, k] numbers a latent block within latent shard s; the 2 entries of one token block and shard are distinct, and those with k >= block_counts[b, s] are inactive slots. block_counts[b, s] is how many leading slots of block_ids[b, s] are active; some entry equals 2 in every draw.
All inputs are finite; a program needn't handle non-finite values.
Results may differ from the reference program's by a relative error of at most 0.02.
Values may be sent and summed in bfloat16 or wider, within the bound.
No kernel may reach another device: no remote copies, remote signals or barrier semaphores. Data moves between devices by JAX's collectives and lax.ppermute only.
A program may use at most 128 MiB of HBM per device.

```python
import jax
import jax.numpy as jnp
from jax import lax

L = 16384
TB = 128
LB = 128
KS = 2
F = 16384
TOKENS = 4096
NTB = 32
LBD = 16
ACTIVE = 2048
N_LAT = 8


def pick_row(row_key):
    return jax.random.permutation(row_key, LBD)[:KS]


def draw_block_ids(key, part):
    row_keys = jax.random.split(jax.random.fold_in(key, 11), NTB * N_LAT)
    chosen = jax.vmap(pick_row)(row_keys)
    return chosen.reshape(NTB, N_LAT, KS).astype(jnp.int32)


def draw_block_counts(key, part):
    base_key = jax.random.fold_in(key, 23)
    key_level, key_extra, key_row, key_col = jax.random.split(base_key, 4)
    levels = jax.random.randint(key_level, (N_LAT,), 0, KS)
    extra_slots = jax.random.randint(key_extra, (NTB, N_LAT), 0, KS)
    counts = 1 + jnp.minimum(extra_slots, levels[None, :])
    row_at = jax.random.randint(key_row, (), 0, NTB)
    col_at = jax.random.randint(key_col, (), 0, N_LAT)
    return counts.at[row_at, col_at].set(KS).astype(jnp.int32)


def level_of(key, shape, shards, least, high):
    def one(dim, parts):
        heights = jax.random.uniform(jax.random.fold_in(jax.random.fold_in(key, 6), dim), (parts,), jnp.float32, least / len(shards), high / len(shards))
        return jnp.repeat(jnp.exp(heights), shape[dim] // parts).reshape((-1,) + (1,) * (len(shape) - dim - 1))

    loudness = one(*shards[0])
    for cut in shards[1:]:
        loudness = loudness * one(*cut)
    return loudness


def bell_draw(key, shape, deviation, reach, shards=(), kind=jnp.bfloat16):
    level = level_of(key, shape, shards, -0.22, 0.18) if shards else 1.0
    drawn = jax.random.normal(key, shape, jnp.float32) * deviation * level
    return jnp.minimum(jnp.maximum(drawn, -reach), reach).astype(kind)


def setup_inputs(seed: int = 0) -> dict:
    streams_of = jax.random.split(jax.random.key(seed), 8)
    captured = bell_draw(streams_of[0], (TOKENS, F), 1.0, 6.0, ((1, 32),))
    enc_weight = bell_draw(streams_of[1], (F, L), F ** -0.5, 0.046875, ((0, 32), (1, 8)))
    enc_bias = bell_draw(streams_of[2], (L,), 0.5, 3.0, ((0, 8),), jnp.float32)
    dec_weight = bell_draw(streams_of[3], (L, F), ACTIVE ** -0.5, 0.125, ((0, 8), (1, 32)))
    dec_bias = bell_draw(streams_of[4], (F,), 0.25, 1.5, ((0, 32),), jnp.float32)
    block_ids = draw_block_ids(jax.random.fold_in(streams_of[7], 71), 0)
    block_counts = draw_block_counts(jax.random.fold_in(streams_of[7], 71), 0)
    return dict(captured=captured, enc_weight=enc_weight, enc_bias=enc_bias, dec_weight=dec_weight, dec_bias=dec_bias, block_ids=block_ids, block_counts=block_counts)


SCALE_ERR = 0.0625
PENALTY = 0.05


def reference(captured, enc_weight, enc_bias, dec_weight, dec_bias, block_ids, block_counts):
    features = captured.shape[1]
    all_blocks = captured.shape[0] // TB
    lat_blocks = L // LB
    slots = N_LAT * KS
    enc_cube = enc_weight.reshape(features, lat_blocks, LB)
    dec_cube = dec_weight.reshape(lat_blocks, LB, features)
    bias_cube = enc_bias.reshape(lat_blocks, LB)
    offsets = (jnp.arange(N_LAT, dtype=jnp.int32) * LBD)[:, None]
    rows_all = captured.reshape(all_blocks, TB, features)

    def one_block(inputs):
        rows_in, ids_row, counts_row = inputs
        global_ids = (offsets + ids_row).reshape(slots).astype(jnp.int32)
        enc_tiles = jnp.take(enc_cube, global_ids, axis=1).astype(jnp.float32)
        pre_act = jnp.einsum("tf,fmc->mtc", rows_in.astype(jnp.float32), enc_tiles)
        pre_act = pre_act + jnp.take(bias_cube, global_ids, axis=0)[:, None, :]
        live_slots = (jnp.arange(KS, dtype=jnp.int32)[None, :] < counts_row[:, None]).reshape(slots)
        codes = (jax.nn.softplus(pre_act) * live_slots.astype(jnp.float32)[:, None, None]).astype(jnp.bfloat16)
        dec_tiles = jnp.take(dec_cube, global_ids, axis=0).astype(jnp.float32)
        partial_value = jnp.einsum("lktc,lkcf->ltf", codes.astype(jnp.float32).reshape(N_LAT, KS, TB, LB),
                             dec_tiles.reshape(N_LAT, KS, LB, features))
        partial_value = lax.optimization_barrier(partial_value.astype(jnp.bfloat16)).astype(jnp.float32)
        rebuilt = jnp.sum(partial_value, axis=0)
        err_grad = SCALE_ERR * (rebuilt + dec_bias[None, :] - rows_in.astype(jnp.float32))
        err_half = err_grad.astype(jnp.bfloat16)
        code_grads = jnp.einsum("tf,mcf->mtc", err_half.astype(jnp.float32), dec_tiles)
        pre_grads = ((code_grads + PENALTY) * (1.0 - jnp.exp(-codes.astype(jnp.float32)))).astype(jnp.bfloat16)
        return codes, err_half, pre_grads

    codes, err_half, pre_grads = lax.map(one_block, (rows_all, block_ids, block_counts))
    codes_shard = codes.reshape(all_blocks, N_LAT, KS, TB, LB).transpose(1, 0, 2, 3, 4)
    grads_shard = pre_grads.reshape(all_blocks, N_LAT, KS, TB, LB).transpose(1, 0, 2, 3, 4)
    ids_shard = block_ids.transpose(1, 0, 2)

    def one_shard(inputs):
        shard_codes, shard_grads, shard_ids = inputs

        def step(carry, item):
            dec_acc, enc_acc = carry
            code_tiles, grad_tiles, chosen, rows_in, err_rows = item
            tile_dec = jnp.einsum("ktc,tf->kcf", code_tiles.astype(jnp.float32), err_rows.astype(jnp.float32))
            tile_enc = jnp.einsum("tf,ktc->fkc", rows_in.astype(jnp.float32), grad_tiles.astype(jnp.float32))
            return (dec_acc.at[chosen].add(tile_dec), enc_acc.at[:, chosen].add(tile_enc)), None

        start_acc = (jnp.zeros((LBD, LB, features), jnp.float32), jnp.zeros((features, LBD, LB), jnp.float32))
        (dec_acc, enc_acc), unused = lax.scan(step, start_acc, (shard_codes, shard_grads, shard_ids, rows_all, err_half))
        return (dec_acc.reshape(LBD * LB, features).astype(jnp.bfloat16),
                enc_acc.reshape(features, LBD * LB).astype(jnp.bfloat16))

    dec_parts, enc_parts = lax.map(one_shard, (codes_shard, grads_shard, ids_shard))
    dec_grad = dec_parts.reshape(L, features)
    enc_grad = enc_parts.transpose(1, 0, 2).reshape(features, L)
    return enc_grad, dec_grad
```

```python
import functools

import jax
import jax.numpy as jnp
from jax import lax
from jax.experimental import pallas as pl
from jax.experimental.pallas import tpu as pltpu
from jax.sharding import Mesh, PartitionSpec as P

TB = 128
LB = 128
KS = 2
NTB = 32
NY, NX, NC, NZ = 4, 4, 2, 8
CHIPS = NY * NX
GROUPS = 1
NB = NTB // GROUPS
BPC = NB // CHIPS
BPZ = NB // NZ
HALF = BPZ // 2 * TB

SCALE_ERR = 0.0625
PENALTY = 0.05

BF = jnp.bfloat16
F32 = jnp.float32
VMEM_LIMIT = 40 * 1024 * 1024

COUNTS, CORE, CHIP, ZPOS = NTB * KS, NTB * KS + NTB, NTB * KS + NTB + 1, NTB * KS + NTB + 2

SMEM = pl.BlockSpec(memory_space=pltpu.SMEM)
VMEM = pl.BlockSpec(memory_space=pltpu.VMEM)


def params():
    return pltpu.CompilerParams(vmem_limit_bytes=VMEM_LIMIT)


def cost(flops, nbytes):
    return pl.CostEstimate(flops=flops, bytes_accessed=nbytes, transcendentals=0)


def rows_of(block):
    return pl.ds(pl.multiple_of(block * TB, TB), TB)


def pair_of(meta, gid):
    core = meta[CORE]
    return meta[KS * gid + core], meta[KS * gid + 1 - core]


def enc_kernel(first, step_blocks, meta, cap, enc, mine, theirs):
    base = first + pl.program_id(0) * step_blocks

    def body(b, carry):
        ia, ib = pair_of(meta, base + b)
        w = jnp.concatenate([enc[:, rows_of(ia)], enc[:, rows_of(ib)]], axis=1)
        out = jnp.dot(cap[rows_of(b), :], w, preferred_element_type=F32).astype(BF)
        mine[rows_of(b), :] = out[:, :LB]
        theirs[rows_of(b), :] = out[:, LB:]
        return carry

    lax.fori_loop(0, step_blocks, body, 0, unroll=2)


def encode(group, meta, captured, enc):
    steps = 4
    sb = NB // steps
    feats = captured.shape[1]
    out = jax.ShapeDtypeStruct((NB * TB, LB), BF)
    spec = pl.BlockSpec((sb * TB, LB), lambda i: (i, 0))
    return pl.pallas_call(
        functools.partial(enc_kernel, group * NB, sb),
        grid=(steps,),
        in_specs=[
            SMEM,
            pl.BlockSpec((sb * TB, feats), lambda i: (group * steps + i, 0)),
            pl.BlockSpec(enc.shape, lambda i: (0, 0)),
        ],
        out_specs=[spec, spec],
        out_shape=[out, out],
        compiler_params=params(),
        cost_estimate=cost(2 * NB * TB * feats * KS * LB, NB * TB * (feats + 256) * 2 + enc.size * 2),
        name="encode",
    )(meta, captured, enc)


def codes_kernel(first, meta, terms, bias, copies, own):
    for q in range(BPC):
        gid = first + meta[CHIP] * BPC + q
        core = meta[CORE]
        row = bias[pl.ds(meta[KS * gid + core], 1), :]
        v = jnp.sum(terms[:, q * TB : (q + 1) * TB, :].astype(F32), axis=0) + row
        soft = jnp.maximum(v, 0.0) + jnp.log1p(jnp.exp(-jnp.abs(v)))
        code = jnp.where(core < meta[COUNTS + gid], soft, 0.0).astype(BF)
        own[q * TB : (q + 1) * TB, :] = code
        for chip in range(CHIPS):
            copies[chip, q * TB : (q + 1) * TB, :] = code


def make_codes(group, meta, terms, bias):
    return pl.pallas_call(
        functools.partial(codes_kernel, group * NB),
        in_specs=[SMEM, VMEM, VMEM],
        out_specs=[VMEM, VMEM],
        out_shape=[jax.ShapeDtypeStruct(terms.shape, BF), jax.ShapeDtypeStruct(terms.shape[1:], BF)],
        compiler_params=params(),
        cost_estimate=cost(20 * terms.size, 4 * terms.size),
        name="codes",
    )(meta, terms, bias)


def dpre_kernel(terms, own, copies):
    total = jnp.sum(terms[...].astype(F32), axis=0)
    grad = ((total + PENALTY) * (1.0 - jnp.exp(-own[...].astype(F32)))).astype(BF)
    for chip in range(CHIPS):
        copies[chip] = grad


def make_dpre(terms, own):
    return pl.pallas_call(
        dpre_kernel,
        in_specs=[VMEM, VMEM],
        out_specs=VMEM,
        out_shape=jax.ShapeDtypeStruct(terms.shape, BF),
        compiler_params=params(),
        cost_estimate=cost(20 * terms.size, 4 * terms.size),
        name="dpre",
    )(terms, own)


ORDER = (0, 1, 7, 2, 6, 3, 5, 4)


def piece_shapes(feats):
    full = jax.ShapeDtypeStruct((BPZ * TB, feats), BF)
    half = jax.ShapeDtypeStruct((HALF, feats), BF)
    return [full] * 7 + [half, half]


def piece_at(pieces, slot, j):
    if slot < 7:
        return pieces[slot], j * TB
    if j * TB < HALF:
        return pieces[7], j * TB
    return pieces[8], j * TB - HALF


def part_kernel(first, meta, mine, other, dec, *pieces):
    for slot, ahead in enumerate(ORDER):
        chunk = lax.rem(meta[ZPOS] + ahead, NZ)
        for j in range(BPZ):
            b = chunk * BPZ + j
            ia, ib = pair_of(meta, first + b)
            codes = jnp.concatenate([mine[rows_of(b), :], other[rows_of(b), :]], axis=1)
            w = jnp.concatenate([dec[rows_of(ia), :], dec[rows_of(ib), :]], axis=0)
            piece, row = piece_at(pieces, slot, j)
            piece[row : row + TB, :] = jnp.dot(codes, w, preferred_element_type=F32).astype(BF)


def make_parts(group, meta, mine, other, dec):
    feats = dec.shape[1]
    shapes = piece_shapes(feats)
    return pl.pallas_call(
        functools.partial(part_kernel, group * NB),
        in_specs=[SMEM, VMEM, VMEM, VMEM],
        out_specs=[VMEM] * 9,
        out_shape=shapes,
        compiler_params=params(),
        cost_estimate=cost(2 * NB * TB * feats * KS * LB, NB * TB * (feats + 256) * 2 + dec.size * 2),
        name="parts",
    )(meta, mine, other, dec)


def add_kernel(n, *refs):
    for i in range(n):
        a, b, o = refs[2 * i], refs[2 * i + 1], refs[2 * n + i]
        o[...] = (a[...].astype(F32) + b[...].astype(F32)).astype(BF)


def add_first_kernel(pa, ra, pb, rb, oa, ob):
    oa[:HALF, :] = (pa[:HALF, :].astype(F32) + ra[...].astype(F32)).astype(BF)
    oa[HALF:, :] = pa[HALF:, :]
    ob[:HALF, :] = pb[:HALF, :]
    ob[HALF:, :] = (pb[HALF:, :].astype(F32) + rb[...].astype(F32)).astype(BF)


def add_both(kernel, pa, ra, pb, rb):
    out = jax.ShapeDtypeStruct(pa.shape, BF)
    return pl.pallas_call(
        kernel,
        in_specs=[VMEM] * 4,
        out_specs=[VMEM] * 2,
        out_shape=[out, out],
        compiler_params=params(),
        cost_estimate=cost(2 * pa.size, 12 * pa.size),
        name="ring_add",
    )(pa, ra, pb, rb)


def delta_kernel(meta, part, ra, rb, bias, cap, out):
    rec = part[...].astype(F32) + ra[...].astype(F32) + rb[...].astype(F32)
    out[...] = (SCALE_ERR * (rec + bias[...] - cap[...].astype(F32))).astype(BF)


def make_delta(group, meta, part, ra, rb, bias, captured):
    feats = captured.shape[1]
    rows = BPZ * TB
    block = pl.BlockSpec((rows, feats), lambda i, meta: (0, 0))
    return pl.pallas_call(
        delta_kernel,
        grid_spec=pltpu.PrefetchScalarGridSpec(
            num_scalar_prefetch=1,
            grid=(1,),
            in_specs=[
                block,
                block,
                block,
                pl.BlockSpec((1, feats), lambda i, meta: (0, 0)),
                pl.BlockSpec((rows, feats), lambda i, meta: (group * NZ + meta[ZPOS], 0)),
            ],
            out_specs=block,
        ),
        out_shape=jax.ShapeDtypeStruct((rows, feats), BF),
        compiler_params=params(),
        cost_estimate=cost(6 * rows * feats, 10 * rows * feats),
        name="delta",
    )(meta, part, ra, rb, bias, captured)


RIGHT = [(i, (i + 1) % NZ) for i in range(NZ)]
LEFT = [(i, (i - 1) % NZ) for i in range(NZ)]
SWAP = [(0, 1), (1, 0)]


def to_right(x):
    return lax.ppermute(x, "lat", RIGHT)


def to_left(x):
    return lax.ppermute(x, "lat", LEFT)


def reduce_z(group, meta, pieces, bias, captured):
    r, l = to_right(pieces[7]), to_left(pieces[8])
    a, b = add_both(add_first_kernel, pieces[5], r, pieces[6], l)
    r, l = to_right(a), to_left(b)
    for slot in (3, 1):
        a, b = add_both(functools.partial(add_kernel, 2), pieces[slot], r, pieces[slot + 1], l)
        r, l = to_right(a), to_left(b)
    return make_delta(group, meta, pieces[0], r, l, bias, captured)


def gather_z(own):
    out = [own]
    r = l = own
    for _ in range(3):
        r, l = to_right(r), to_left(l)
        out += [l, r]
    half = own.shape[0] // 2
    return out + [to_right(r[:half]), to_left(l[half:])]


def dcodes_kernel(first, meta, dec, *refs):
    pieces, (mine, theirs) = refs[:9], refs[9:]
    for slot, ahead in enumerate(ORDER):
        chunk = lax.rem(meta[ZPOS] + ahead, NZ)
        for j in range(BPZ):
            b = chunk * BPZ + j
            ia, ib = pair_of(meta, first + b)
            w = jnp.concatenate([dec[rows_of(ia), :], dec[rows_of(ib), :]], axis=0)
            piece, row = piece_at(pieces, slot, j)
            out = lax.dot_general(
                piece[row : row + TB, :], w, (((1,), (1,)), ((), ())), preferred_element_type=F32
            ).astype(BF)
            mine[rows_of(b), :] = out[:, :LB]
            theirs[rows_of(b), :] = out[:, LB:]


def make_dcodes(group, meta, dec, pieces):
    feats = dec.shape[1]
    out = jax.ShapeDtypeStruct((NB * TB, LB), BF)
    return pl.pallas_call(
        functools.partial(dcodes_kernel, group * NB),
        in_specs=[SMEM] + [VMEM] * 10,
        out_specs=[VMEM, VMEM],
        out_shape=[out, out],
        compiler_params=params(),
        cost_estimate=cost(2 * NB * TB * feats * KS * LB, NB * TB * (feats + 256) * 2 + dec.size * 2),
        name="dcodes",
    )(meta, dec, *pieces)


def dec_grad_kernel(meta, *refs):
    out, acc = refs[-2:]
    acc[...] = jnp.zeros_like(acc)
    for g in range(GROUPS):
        mine, other = refs[11 * g : 11 * g + 2]
        pieces = refs[11 * g + 2 : 11 * g + 11]
        for slot, ahead in enumerate(ORDER):
            chunk = lax.rem(meta[ZPOS] + ahead, NZ)
            for j in range(BPZ):
                b = chunk * BPZ + j
                ia, ib = pair_of(meta, g * NB + b)
                codes = jnp.concatenate([mine[rows_of(b), :], other[rows_of(b), :]], axis=1)
                piece, row = piece_at(pieces, slot, j)
                prod = lax.dot_general(
                    codes, piece[row : row + TB, :], (((0,), (0,)), ((), ())), preferred_element_type=F32
                )
                acc[rows_of(ia), :] += prod[:LB]
                acc[rows_of(ib), :] += prod[LB:]
    out[...] = acc[...].astype(BF)


def make_dec_grad(meta, shape, groups):
    args = [a for mine, other, pieces in groups for a in (mine, other, *pieces)]
    return pl.pallas_call(
        dec_grad_kernel,
        in_specs=[SMEM] + [VMEM] * len(args),
        out_specs=VMEM,
        out_shape=jax.ShapeDtypeStruct(shape, BF),
        scratch_shapes=[pltpu.VMEM(shape, F32)],
        compiler_params=params(),
        cost_estimate=cost(2 * NTB * TB * shape[1] * KS * LB, NTB * TB * (shape[1] + 256) * 2 + shape[0] * shape[1] * 2),
        name="dec_grad",
    )(meta, *args)


def enc_grad_kernel(meta, cap, *refs):
    out, acc = refs[-2:]
    acc[...] = jnp.zeros_like(acc)
    for g in range(GROUPS):
        mine, other = refs[2 * g : 2 * g + 2]

        def body(b, carry):
            gid = g * NB + b
            ia, ib = pair_of(meta, gid)
            grads = jnp.concatenate([mine[rows_of(b), :], other[rows_of(b), :]], axis=1)
            prod = lax.dot_general(
                cap[rows_of(gid), :], grads, (((0,), (0,)), ((), ())), preferred_element_type=F32
            )
            acc[ia] += prod[:, :LB]
            acc[ib] += prod[:, LB:]
            return carry

        lax.fori_loop(0, NB, body, 0, unroll=2)
    for i in range(acc.shape[0]):
        out[:, i * LB : (i + 1) * LB] = acc[i].astype(BF)


def make_enc_grad(meta, captured, shape, groups):
    args = [a for pair in groups for a in pair]
    return pl.pallas_call(
        enc_grad_kernel,
        in_specs=[SMEM] + [VMEM] * (1 + len(args)),
        out_specs=VMEM,
        out_shape=jax.ShapeDtypeStruct(shape, BF),
        scratch_shapes=[pltpu.VMEM((shape[1] // LB, shape[0], LB), F32)],
        compiler_params=params(),
        cost_estimate=cost(2 * NTB * TB * shape[0] * KS * LB, NTB * TB * (shape[0] + 256) * 2 + shape[0] * shape[1] * 2),
        name="enc_grad",
    )(meta, captured, *args)


def tok_scatter(mine, theirs):
    got = lax.ppermute(theirs, "core", SWAP)
    pair = (mine.astype(F32) + got.astype(F32)).astype(BF)
    return lax.all_to_all(pair.reshape(CHIPS, BPC * TB, LB), ("y", "x"), 0, 0, tiled=True)


def tok_gather(copies):
    mine = lax.all_to_all(copies, ("y", "x"), 0, 0, tiled=True).reshape(NB * TB, LB)
    return mine, lax.ppermute(mine, "core", SWAP)


def local(captured, enc_weight, enc_bias, dec_weight, dec_bias, block_ids, block_counts):
    chip = lax.axis_index(("y", "x"))
    place = jnp.stack([lax.axis_index("core"), chip, lax.axis_index("lat")]).astype(jnp.int32)
    meta = jnp.concatenate([block_ids.reshape(-1), block_counts.reshape(-1), place])
    enc_bias = enc_bias.reshape(-1, LB)
    dec_bias = dec_bias.reshape(1, -1)

    codes, deltas, dpres = [], [], []
    for g in range(GROUPS):
        terms = tok_scatter(*encode(g, meta, captured, enc_weight))
        copies, own = make_codes(g, meta, terms, enc_bias)
        mine, other = tok_gather(copies)
        pieces = make_parts(g, meta, mine, other, dec_weight)
        delta = reduce_z(g, meta, pieces, dec_bias, captured)
        deltas.append(gather_z(delta))
        codes.append((mine, other))
        terms = tok_scatter(*make_dcodes(g, meta, dec_weight, deltas[g]))
        dpres.append(tok_gather(make_dpre(terms, own)))
    dec_grad = make_dec_grad(meta, dec_weight.shape, [(*codes[g], deltas[g]) for g in range(GROUPS)])
    enc_grad = make_enc_grad(meta, captured, enc_weight.shape, dpres)
    return enc_grad, dec_grad


def solution(mesh):
    cube = Mesh(mesh.devices.reshape(NY, NX, NC, NZ), ("y", "x", "core", "lat"))
    tok = ("y", "x", "core")
    in_specs = (
        P(None, tok),
        P(tok, "lat"),
        P("lat"),
        P("lat", tok),
        P(tok),
        P(None, "lat", None),
        P(None, "lat"),
    )
    out_specs = (P(tok, "lat"), P("lat", tok))
    return jax.shard_map(local, mesh=cube, in_specs=in_specs, out_specs=out_specs, check_vma=False)
```

```python
import functools

import jax
import jax.numpy as jnp
from jax import lax
from jax.experimental import pallas as pl
from jax.experimental.pallas import tpu as pltpu
from jax.sharding import Mesh, PartitionSpec as P

TB = 128
LB = 128
KS = 2
NTB = 32
NY, NX, NC, NZ = 4, 4, 2, 8
SIDE = 4
CHAINS = 2
QB = NTB // SIDE
OB = QB // SIDE
ZB = NTB // NZ // CHAINS
FULL = ZB * TB
HALF = FULL // 2

SCALE_ERR = 0.0625
PENALTY = 0.05

BF = jnp.bfloat16
F32 = jnp.float32
VMEM_LIMIT = 24 * 1024 * 1024
ENCODE_LIMIT = 60 * 1024 * 1024

COUNTS = NTB * KS
CORE, FIRST, SECOND, ZPOS = (COUNTS + NTB + i for i in range(4))

SMEM = pl.BlockSpec(memory_space=pltpu.SMEM)
VMEM = pl.BlockSpec(memory_space=pltpu.VMEM)
HBM = pl.BlockSpec(memory_space=pltpu.HBM)


def cost(flops, nbytes):
    return pl.CostEstimate(flops=flops, bytes_accessed=nbytes, transcendentals=0)


def call(kernel, name, in_specs, out_shape, args, flops, scratch=(), aliases=None, limit=VMEM_LIMIT):
    outs = out_shape if isinstance(out_shape, list) else [out_shape]
    nbytes = sum(a.size * a.dtype.itemsize for a in (*args, *outs))
    return pl.pallas_call(
        kernel,
        in_specs=in_specs,
        out_specs=[VMEM] * len(out_shape) if isinstance(out_shape, list) else VMEM,
        out_shape=out_shape,
        scratch_shapes=list(scratch),
        input_output_aliases=aliases or {},
        compiler_params=pltpu.CompilerParams(vmem_limit_bytes=limit),
        cost_estimate=cost(flops, nbytes),
        name=name,
    )(*args)


def shape(*dims, dtype=BF):
    return jax.ShapeDtypeStruct(dims, dtype)


def rows_of(block, count=1):
    return pl.ds(pl.multiple_of(block * TB, TB), count * TB)


def pair_of(meta, block):
    core = meta[CORE]
    return meta[KS * block + core], meta[KS * block + 1 - core]


def ring4(place, step):
    return lax.rem(place + step + SIDE, SIDE)


def total(refs, rows=slice(None)):
    out = refs[0][rows, :].astype(F32)
    for ref in refs[1:]:
        out += ref[rows, :].astype(F32)
    return out


MATMUL = 2 * NTB * TB * KS * LB


def enc_kernel(meta, cap_hbm, enc_hbm, mine, theirs, cap, enc, sems):
    n = SIDE
    er, cr = enc.shape[0] // n, cap.shape[0] // n
    copies = [
        pltpu.make_async_copy(enc_hbm.at[pl.ds(i * er, er)], enc.at[pl.ds(i * er, er)], sems.at[i]) for i in range(n)
    ] + [pltpu.make_async_copy(cap_hbm.at[pl.ds(i * cr, cr)], cap.at[pl.ds(i * cr, cr)], sems.at[n + i]) for i in range(n)]
    for copy in copies:
        copy.start()
    for copy in copies[:n]:
        copy.wait()

    def body(b, carry):
        ia, ib = pair_of(meta, b)
        w = jnp.concatenate([enc[:, rows_of(ia)], enc[:, rows_of(ib)]], axis=1)
        out = jnp.dot(cap[rows_of(b), :], w, preferred_element_type=F32).astype(BF)
        mine[rows_of(b), :] = out[:, :LB]
        theirs[rows_of(b), :] = out[:, LB:]
        return carry

    for i in range(n):
        copies[n + i].wait()
        lax.fori_loop(i * (NTB // n), (i + 1) * (NTB // n), body, 0, unroll=4)


def encode(meta, captured, enc):
    out = shape(NTB * TB, LB)
    return call(
        enc_kernel,
        "encode",
        [SMEM, HBM, HBM],
        [out, out],
        (meta, captured, enc),
        MATMUL * enc.shape[0],
        [pltpu.VMEM(captured.shape, BF), pltpu.VMEM(enc.shape, BF), pltpu.SemaphoreType.DMA((2 * SIDE,))],
        limit=ENCODE_LIMIT,
    )


def split_add_kernel(meta, mine, got, *quarters):
    for k in range(SIDE):
        quarters[k][...] = total((mine, got), rows_of(ring4(meta[FIRST], k) * QB, QB)).astype(BF)


def split_sum_kernel(meta, *refs):
    for k in range(SIDE):
        refs[SIDE + k][...] = total(refs[:SIDE], rows_of(ring4(meta[SECOND], k) * OB, OB)).astype(BF)


def join_kernel(meta, *refs):
    for k in range(SIDE):
        refs[SIDE][rows_of(ring4(meta[SECOND], -k) * OB, OB), :] = refs[k][...]


SWAP = [(0, 1), (1, 0)]


def swap(x):
    return lax.ppermute(x, "core", SWAP)


def tok_perm(first, step):
    pairs = []
    for y in range(NY):
        for x in range(NX):
            for c in range(NC):
                ty, tx = (y, (x + step) % NX) if (c == 0) == first else ((y + step) % NY, x)
                pairs.append(((y * NX + x) * NC + c, (ty * NX + tx) * NC + c))
    return pairs


def send(x, first, step):
    return lax.ppermute(x, ("y", "x", "core"), tok_perm(first, step))


def exchange(pieces, first):
    return [pieces[0]] + [send(pieces[k], first, k) for k in (2, 1, 3)]


def tok_scatter(meta, mine, theirs):
    got = swap(theirs)
    quarters = call(
        split_add_kernel, "split_add", [SMEM, VMEM, VMEM], [shape(QB * TB, LB)] * SIDE, (meta, mine, got), mine.size
    )
    terms = exchange(quarters, True)
    pieces = call(
        split_sum_kernel, "split_sum", [SMEM] + [VMEM] * SIDE, [shape(OB * TB, LB)] * SIDE, (meta, *terms), mine.size
    )
    return exchange(pieces, False)


def tok_gather(meta, own):
    parts = [own] + [send(own, False, k) for k in range(1, SIDE)]
    quarter = call(join_kernel, "join", [SMEM] + [VMEM] * SIDE, shape(QB * TB, LB), (meta, *parts), own.size)
    mine = [quarter] + [send(quarter, True, k) for k in range(1, SIDE)]
    return mine, [swap(q) for q in mine]


def join_slots(meta, mine, other, both):
    for k in range(SIDE):
        both[rows_of(ring4(meta[FIRST], -k) * QB, QB), :LB] = mine[k][...]
        both[rows_of(ring4(meta[SECOND], -k) * QB, QB), LB:] = other[k][...]


def codes_kernel(meta, *refs):
    terms, (bias, own) = refs[:SIDE], refs[SIDE:]
    core = meta[CORE]
    for q in range(OB):
        block = meta[FIRST] * QB + meta[SECOND] * OB + q
        rows = slice(q * TB, (q + 1) * TB)
        v = total(terms, rows) + bias[pl.ds(meta[KS * block + core], 1), :]
        soft = jnp.maximum(v, 0.0) + jnp.log1p(jnp.exp(-jnp.abs(v)))
        own[rows, :] = jnp.where(core < meta[COUNTS + block], soft, 0.0).astype(BF)


def dpre_kernel(*refs):
    terms, (own, out) = refs[:SIDE], refs[SIDE:]
    out[...] = ((total(terms) + PENALTY) * (1.0 - jnp.exp(-own[...].astype(F32)))).astype(BF)


ORDER = (0, 1, 7, 2, 6, 3, 5, 4, 4)
NP = len(ORDER)


def piece_shapes(feats):
    return [shape(FULL, feats)] * 7 + [shape(HALF, feats)] * 2


def blocks_of(meta, pieces, slots=range(NP)):
    for slot in slots:
        chunk = lax.rem(meta[ZPOS] + ORDER[slot], NZ)
        for chain in range(CHAINS):
            ref = pieces[chain * NP + slot]
            base = chunk * ZB * CHAINS + chain * ZB + (ZB // 2 if slot == 8 else 0)
            for j in range(ref.shape[0] // TB):
                yield base + j, ref, slice(j * TB, (j + 1) * TB)


def dec_rows(meta, dec, block):
    ia, ib = pair_of(meta, block)
    return jnp.concatenate([dec[rows_of(ia), :], dec[rows_of(ib), :]], axis=0)


def part_kernel(meta, dec, *refs):
    both, pieces = refs[2 * SIDE], refs[2 * SIDE + 1 :]
    join_slots(meta, refs[:SIDE], refs[SIDE : 2 * SIDE], both)
    for block, piece, rows in blocks_of(meta, pieces, (7, 8, 5, 6, 3, 4, 1, 2, 0)):
        out = jnp.dot(both[rows_of(block), :], dec_rows(meta, dec, block), preferred_element_type=F32)
        piece[rows, :] = out.astype(BF)


def make_parts(meta, mine, other, dec):
    feats = dec.shape[1]
    outs = call(
        part_kernel,
        "parts",
        [SMEM] + [VMEM] * (1 + 2 * SIDE),
        [shape(NTB * TB, KS * LB)] + piece_shapes(feats) * CHAINS,
        (meta, dec, *mine, *other),
        MATMUL * feats,
    )
    return outs[0], [outs[1 + c * NP : 1 + (c + 1) * NP] for c in range(CHAINS)]


def add_kernel(pa, ra, pb, rb, oa, ob):
    oa[...] = total((pa, ra)).astype(BF)
    ob[...] = total((pb, rb)).astype(BF)


def add_first_kernel(pa, ra, pb, rb, oa, ob):
    oa[:HALF, :] = (pa[:HALF, :].astype(F32) + ra[...].astype(F32)).astype(BF)
    oa[HALF:, :] = pa[HALF:, :]
    ob[:HALF, :] = pb[:HALF, :]
    ob[HALF:, :] = (pb[HALF:, :].astype(F32) + rb[...].astype(F32)).astype(BF)


def add_both(kernel, *args):
    return call(kernel, "ring_add", [VMEM] * 4, [shape(*args[0].shape)] * 2, args, args[0].size)


def delta_kernel(chain, meta, part, ra, rb, bias, cap, out):
    rows = rows_of((meta[ZPOS] * CHAINS + chain) * ZB, ZB)
    rec = total((part, ra, rb))
    out[...] = (SCALE_ERR * (rec + bias[...] - cap[rows, :].astype(F32))).astype(BF)


RIGHT = [(i, (i + 1) % NZ) for i in range(NZ)]
LEFT = [(i, (i - 1) % NZ) for i in range(NZ)]


def to_right(x):
    return lax.ppermute(x, "lat", RIGHT)


def to_left(x):
    return lax.ppermute(x, "lat", LEFT)


def reduce_z(meta, chains, bias, captured):
    moving = [(to_right(p[7]), to_left(p[8])) for p in chains]
    for slot in (5, 3, 1):
        kernel = add_first_kernel if slot == 5 else add_kernel
        sums = [add_both(kernel, p[slot], r, p[slot + 1], l) for p, (r, l) in zip(chains, moving)]
        moving = [(to_right(a), to_left(b)) for a, b in sums]
    return [
        call(
            functools.partial(delta_kernel, c),
            "delta",
            [SMEM] + [VMEM] * 5,
            shape(*p[0].shape),
            (meta, p[0], r, l, bias, captured),
            6 * p[0].size,
        )
        for c, (p, (r, l)) in enumerate(zip(chains, moving))
    ]


def gather_z(deltas):
    out = [[own] for own in deltas]
    moving = [(own, own) for own in deltas]
    for _ in range(3):
        moving = [(to_right(r), to_left(l)) for r, l in moving]
        for pieces, (r, l) in zip(out, moving):
            pieces += [l, r]
    for pieces, (r, l) in zip(out, moving):
        pieces += [to_right(r[:HALF]), to_left(l[HALF:])]
    return [piece for pieces in out for piece in pieces]


def dcodes_kernel(slots, meta, dec, *refs):
    mine, theirs = refs[-2:]
    pieces = refs[: CHAINS * NP]
    for block, piece, rows in blocks_of(meta, pieces, slots):
        out = lax.dot_general(
            piece[rows, :], dec_rows(meta, dec, block), (((1,), (1,)), ((), ())), preferred_element_type=F32
        ).astype(BF)
        mine[rows_of(block), :] = out[:, :LB]
        theirs[rows_of(block), :] = out[:, LB:]


def make_dcodes(meta, dec, pieces):
    out = shape(NTB * TB, LB)
    return call(
        functools.partial(dcodes_kernel, range(NP)),
        "dcodes",
        [SMEM] + [VMEM] * (1 + len(pieces)),
        [out, out],
        (meta, dec, *pieces),
        MATMUL * dec.shape[1],
    )


def dec_grad_kernel(meta, both, *refs):
    pieces, (out, acc) = refs[:-2], refs[-2:]
    acc[...] = jnp.zeros_like(acc)
    for slot in range(NP):
        chunk = lax.rem(meta[ZPOS] + ORDER[slot], NZ)
        for chain in range(CHAINS):
            ref = pieces[chain * NP + slot]
            base = chunk * ZB * CHAINS + chain * ZB + (ZB // 2 if slot == 8 else 0)

            def body(j, carry, ref=ref, base=base):
                ia, ib = pair_of(meta, base + j)
                prod = lax.dot_general(
                    both[rows_of(base + j), :], ref[rows_of(j), :], (((0,), (0,)), ((), ())), preferred_element_type=F32
                )
                acc[rows_of(ia), :] += prod[:LB]
                acc[rows_of(ib), :] += prod[LB:]
                return carry

            lax.fori_loop(0, ref.shape[0] // TB, body, 0)
    out[...] = acc[...].astype(BF)


def make_dec_grad(meta, like, both, pieces):
    return call(
        dec_grad_kernel,
        "dec_grad",
        [SMEM] + [VMEM] * (1 + len(pieces)),
        shape(*like.shape),
        (meta, both, *pieces),
        MATMUL * like.shape[1],
        [pltpu.VMEM(like.shape, F32)],
    )


def enc_grad_kernel(meta, cap, *refs):
    out, both, acc = refs[2 * SIDE :]
    join_slots(meta, refs[:SIDE], refs[SIDE : 2 * SIDE], both)
    acc[...] = jnp.zeros_like(acc)

    def body(b, carry):
        ia, ib = pair_of(meta, b)
        prod = lax.dot_general(
            both[rows_of(b), :], cap[rows_of(b), :], (((0,), (0,)), ((), ())), preferred_element_type=F32
        )
        acc[rows_of(ia), :] += prod[:LB]
        acc[rows_of(ib), :] += prod[LB:]
        return carry

    lax.fori_loop(0, NTB, body, 0, unroll=4)
    for i in range(acc.shape[0] // LB):
        tile = slice(i * LB, (i + 1) * LB)
        out[:, tile] = acc[tile, :].T.astype(BF)


def make_enc_grad(meta, captured, like, mine, other):
    return call(
        enc_grad_kernel,
        "enc_grad",
        [SMEM] + [VMEM] * (1 + 2 * SIDE),
        shape(*like.shape),
        (meta, captured, *mine, *other),
        MATMUL * like.shape[0],
        [pltpu.VMEM((NTB * TB, KS * LB), BF), pltpu.VMEM(like.shape[::-1], F32)],
    )


def local(captured, enc_weight, enc_bias, dec_weight, dec_bias, block_ids, block_counts):
    y, x, core = (lax.axis_index(a) for a in ("y", "x", "core"))
    first, second = jnp.where(core == 0, x, y), jnp.where(core == 0, y, x)
    place = jnp.stack([core, first, second, lax.axis_index("lat")]).astype(jnp.int32)
    meta = jnp.concatenate([block_ids.reshape(-1), block_counts.reshape(-1), place])

    terms = tok_scatter(meta, *encode(meta, captured, enc_weight))
    codes = call(
        codes_kernel,
        "codes",
        [SMEM] + [VMEM] * (SIDE + 1),
        shape(*terms[0].shape),
        (meta, *terms, enc_bias.reshape(-1, LB)),
        20 * terms[0].size,
    )
    both, chains = make_parts(meta, *tok_gather(meta, codes), dec_weight)
    pieces = gather_z(reduce_z(meta, chains, dec_bias.reshape(1, -1), captured))
    terms = tok_scatter(meta, *make_dcodes(meta, dec_weight, pieces))
    dec_grad = make_dec_grad(meta, dec_weight, both, pieces)
    dpre = call(
        dpre_kernel, "dpre", [VMEM] * (SIDE + 1), shape(*codes.shape), (*terms, codes), 20 * codes.size
    )
    enc_grad = make_enc_grad(meta, captured, enc_weight, *tok_gather(meta, dpre))
    return enc_grad, dec_grad


def solution(mesh):
    cube = Mesh(mesh.devices.reshape(NY, NX, NC, NZ), ("y", "x", "core", "lat"))
    tok = ("y", "x", "core")
    in_specs = (
        P(None, tok),
        P(tok, "lat"),
        P("lat"),
        P("lat", tok),
        P(tok),
        P(None, "lat", None),
        P(None, "lat"),
    )
    out_specs = (P(tok, "lat"), P("lat", tok))
    return jax.shard_map(local, mesh=cube, in_specs=in_specs, out_specs=out_specs, check_vma=False)
```

```python
import functools

import jax
import jax.numpy as jnp
from jax import lax
from jax.experimental import pallas as pl
from jax.experimental.pallas import tpu as pltpu
from jax.sharding import Mesh, PartitionSpec as P

TB = 128
LB = 128
KS = 2
NTB = 32
NY, NX, NC, NZ = 4, 4, 2, 8
SIDE = 4
CHAINS = 2
QB = NTB // SIDE
ZB = NTB // NZ // CHAINS
FULL = ZB * TB
HALF = FULL // 2

SCALE_ERR = 0.0625
PENALTY = 0.05

BF = jnp.bfloat16
F32 = jnp.float32
VMEM_LIMIT = 24 * 1024 * 1024
ENCODE_LIMIT = 60 * 1024 * 1024

COUNTS = NTB * KS
CORE, FIRST, SECOND, ZPOS = (COUNTS + NTB + i for i in range(4))

SMEM = pl.BlockSpec(memory_space=pltpu.SMEM)
VMEM = pl.BlockSpec(memory_space=pltpu.VMEM)
HBM = pl.BlockSpec(memory_space=pltpu.HBM)


def cost(flops, nbytes):
    return pl.CostEstimate(flops=flops, bytes_accessed=nbytes, transcendentals=0)


def call(kernel, name, in_specs, out_shape, args, flops, scratch=(), aliases=None, limit=VMEM_LIMIT):
    outs = out_shape if isinstance(out_shape, list) else [out_shape]
    nbytes = sum(a.size * a.dtype.itemsize for a in (*args, *outs))
    return pl.pallas_call(
        kernel,
        in_specs=in_specs,
        out_specs=[VMEM] * len(out_shape) if isinstance(out_shape, list) else VMEM,
        out_shape=out_shape,
        scratch_shapes=list(scratch),
        input_output_aliases=aliases or {},
        compiler_params=pltpu.CompilerParams(vmem_limit_bytes=limit),
        cost_estimate=cost(flops, nbytes),
        name=name,
    )(*args)


def shape(*dims, dtype=BF):
    return jax.ShapeDtypeStruct(dims, dtype)


def rows_of(block, count=1):
    return pl.ds(pl.multiple_of(block * TB, TB), count * TB)


def pair_of(meta, block):
    core = meta[CORE]
    return meta[KS * block + core], meta[KS * block + 1 - core]


def ring4(place, step):
    return lax.rem(place + step + SIDE, SIDE)


def total(refs, rows=slice(None)):
    out = refs[0][rows, :].astype(F32)
    for ref in refs[1:]:
        out += ref[rows, :].astype(F32)
    return out


MATMUL = 2 * NTB * TB * KS * LB


def enc_kernel(meta, cap_hbm, enc_hbm, mine, theirs, cap, enc, sems):
    n = SIDE
    er, cr = enc.shape[0] // n, cap.shape[0] // n
    copies = [
        pltpu.make_async_copy(enc_hbm.at[pl.ds(i * er, er)], enc.at[pl.ds(i * er, er)], sems.at[i]) for i in range(n)
    ] + [pltpu.make_async_copy(cap_hbm.at[pl.ds(i * cr, cr)], cap.at[pl.ds(i * cr, cr)], sems.at[n + i]) for i in range(n)]
    for copy in copies:
        copy.start()
    for copy in copies[:n]:
        copy.wait()

    def body(b, carry):
        ia, ib = pair_of(meta, b)
        w = jnp.concatenate([enc[:, rows_of(ia)], enc[:, rows_of(ib)]], axis=1)
        out = jnp.dot(cap[rows_of(b), :], w, preferred_element_type=F32).astype(BF)
        mine[rows_of(b), :] = out[:, :LB]
        theirs[rows_of(b), :] = out[:, LB:]
        return carry

    for i in range(n):
        copies[n + i].wait()
        lax.fori_loop(i * (NTB // n), (i + 1) * (NTB // n), body, 0, unroll=4)


def encode(meta, captured, enc):
    out = shape(NTB * TB, LB)
    return call(
        enc_kernel,
        "encode",
        [SMEM, HBM, HBM],
        [out, out],
        (meta, captured, enc),
        MATMUL * enc.shape[0],
        [pltpu.VMEM(captured.shape, BF), pltpu.VMEM(enc.shape, BF), pltpu.SemaphoreType.DMA((2 * SIDE,))],
        limit=ENCODE_LIMIT,
    )


def split_add_kernel(meta, mine, got, *quarters):
    for k in range(SIDE):
        quarters[k][...] = total((mine, got), rows_of(ring4(meta[FIRST], k) * QB, QB)).astype(BF)


def total4(refs, rows=slice(None)):
    return total(refs[:2], rows) + total(refs[2:4], rows)


def quarter_sum_kernel(*refs):
    refs[SIDE][...] = total4(refs).astype(BF)


SWAP = [(0, 1), (1, 0)]


def swap(x):
    return lax.ppermute(x, "core", SWAP)


def tok_perm(first, step):
    pairs = []
    for y in range(NY):
        for x in range(NX):
            for c in range(NC):
                ty, tx = (y, (x + step) % NX) if (c == 0) == first else ((y + step) % NY, x)
                pairs.append(((y * NX + x) * NC + c, (ty * NX + tx) * NC + c))
    return pairs


def send(x, first, step):
    return lax.ppermute(x, ("y", "x", "core"), tok_perm(first, step))


def exchange(pieces, first):
    return [pieces[0]] + [send(pieces[k], first, k) for k in (2, 1, 3)]


def tok_scatter(meta, mine, theirs, beside=()):
    got = swap(theirs)
    quarters = call(
        split_add_kernel, "split_add", [SMEM, VMEM, VMEM], [shape(QB * TB, LB)] * SIDE, (meta, mine, got), mine.size
    )
    terms = exchange(quarters, True)
    quarter = call(
        lambda *refs: quarter_sum_kernel(*refs[:SIDE], refs[-1]),
        "quarter_sum",
        [VMEM] * SIDE + [VMEM] * len(beside),
        shape(QB * TB, LB),
        (*terms, *beside),
        mine.size,
    )
    return exchange([quarter] * SIDE, False)


def tok_gather(own):
    mine = [own] + [send(own, True, k) for k in range(1, SIDE)]
    return mine, [swap(q) for q in mine]


def join_slots(meta, mine, other, both):
    for k in range(SIDE):
        both[rows_of(ring4(meta[FIRST], -k) * QB, QB), :LB] = mine[k][...]
        both[rows_of(ring4(meta[SECOND], -k) * QB, QB), LB:] = other[k][...]


def codes_kernel(meta, *refs):
    terms, (bias, own) = refs[:SIDE], refs[SIDE:]
    core = meta[CORE]
    for q in range(QB):
        block = meta[FIRST] * QB + q
        rows = slice(q * TB, (q + 1) * TB)
        v = total4(terms, rows) + bias[pl.ds(meta[KS * block + core], 1), :]
        soft = jnp.maximum(v, 0.0) + jnp.log1p(jnp.exp(-jnp.abs(v)))
        own[rows, :] = jnp.where(core < meta[COUNTS + block], soft, 0.0).astype(BF)


def dpre_kernel(*refs):
    terms, (own, out) = refs[:SIDE], refs[SIDE:]
    out[...] = ((total4(terms) + PENALTY) * (1.0 - jnp.exp(-own[...].astype(F32)))).astype(BF)


ORDER = (0, 1, 7, 2, 6, 3, 5, 4, 4)
NP = len(ORDER)


def piece_shapes(feats):
    return [shape(FULL, feats)] * 7 + [shape(HALF, feats)] * 2


def blocks_of(meta, pieces, slots=range(NP)):
    for slot in slots:
        chunk = lax.rem(meta[ZPOS] + ORDER[slot], NZ)
        for chain in range(CHAINS):
            ref = pieces[chain * NP + slot]
            base = chunk * ZB * CHAINS + chain * ZB + (ZB // 2 if slot == 8 else 0)
            for j in range(ref.shape[0] // TB):
                yield base + j, ref, slice(j * TB, (j + 1) * TB)


def dec_rows(meta, dec, block):
    ia, ib = pair_of(meta, block)
    return jnp.concatenate([dec[rows_of(ia), :], dec[rows_of(ib), :]], axis=0)


def parts_of(meta, dec, both, pieces, slots):
    for block, piece, rows in blocks_of(meta, pieces, slots):
        out = jnp.dot(both[rows_of(block), :], dec_rows(meta, dec, block), preferred_element_type=F32)
        piece[rows, :] = out.astype(BF)


def far_parts_kernel(meta, dec, *refs):
    both, pieces = refs[2 * SIDE], refs[2 * SIDE + 1 :]
    join_slots(meta, refs[:SIDE], refs[SIDE : 2 * SIDE], both)
    pieces = [None] * 7 + list(pieces[:2]) + [None] * 7 + list(pieces[2:])
    parts_of(meta, dec, both, pieces, (7, 8))


def near_parts_kernel(meta, dec, both, *pieces):
    pieces = list(pieces[:7]) + [None] * 2 + list(pieces[7:]) + [None] * 2
    parts_of(meta, dec, both, pieces, (5, 6, 3, 4, 1, 2, 0))


def make_parts(meta, mine, other, dec):
    feats = dec.shape[1]
    shapes = piece_shapes(feats)
    both, *far = call(
        far_parts_kernel,
        "far_parts",
        [SMEM] + [VMEM] * (1 + 2 * SIDE),
        [shape(NTB * TB, KS * LB)] + shapes[7:] * CHAINS,
        (meta, dec, *mine, *other),
        MATMUL * feats // 8,
    )
    near = call(
        near_parts_kernel,
        "near_parts",
        [SMEM] + [VMEM] * 2,
        shapes[:7] * CHAINS,
        (meta, dec, both),
        MATMUL * feats,
    )
    return both, [[*near[c * 7 : c * 7 + 7], *far[c * 2 : c * 2 + 2]] for c in range(CHAINS)]


def add_kernel(pa, ra, pb, rb, oa, ob):
    oa[...] = total((pa, ra)).astype(BF)
    ob[...] = total((pb, rb)).astype(BF)


def add_first_kernel(pa, ra, pb, rb, oa, ob):
    oa[:HALF, :] = (pa[:HALF, :].astype(F32) + ra[...].astype(F32)).astype(BF)
    oa[HALF:, :] = pa[HALF:, :]
    ob[:HALF, :] = pb[:HALF, :]
    ob[HALF:, :] = (pb[HALF:, :].astype(F32) + rb[...].astype(F32)).astype(BF)


def add_both(kernel, *args):
    return call(kernel, "ring_add", [VMEM] * 4, [shape(*args[0].shape)] * 2, args, args[0].size)


def delta_kernel(chain, meta, part, ra, rb, bias, cap, out):
    rows = rows_of((meta[ZPOS] * CHAINS + chain) * ZB, ZB)
    rec = total((part, ra, rb))
    out[...] = (SCALE_ERR * (rec + bias[...] - cap[rows, :].astype(F32))).astype(BF)


RIGHT = [(i, (i + 1) % NZ) for i in range(NZ)]
LEFT = [(i, (i - 1) % NZ) for i in range(NZ)]


def to_right(x):
    return lax.ppermute(x, "lat", RIGHT)


def to_left(x):
    return lax.ppermute(x, "lat", LEFT)


def reduce_z(meta, chains, bias, captured):
    moving = [(to_right(p[7]), to_left(p[8])) for p in chains]
    for slot in (5, 3, 1):
        kernel = add_first_kernel if slot == 5 else add_kernel
        sums = [add_both(kernel, p[slot], r, p[slot + 1], l) for p, (r, l) in zip(chains, moving)]
        moving = [(to_right(a), to_left(b)) for a, b in sums]
    return [
        call(
            functools.partial(delta_kernel, c),
            "delta",
            [SMEM] + [VMEM] * 5,
            shape(*p[0].shape),
            (meta, p[0], r, l, bias, captured),
            6 * p[0].size,
        )
        for c, (p, (r, l)) in enumerate(zip(chains, moving))
    ]


def gather_z(deltas):
    out = [[own] for own in deltas]
    moving = [(own, own) for own in deltas]
    for _ in range(3):
        moving = [(to_right(r), to_left(l)) for r, l in moving]
        for pieces, (r, l) in zip(out, moving):
            pieces += [l, r]
    for pieces, (r, l) in zip(out, moving):
        pieces += [to_right(r[:HALF]), to_left(l[HALF:])]
    return [piece for pieces in out for piece in pieces]


def dcodes_of(meta, dec, pieces, slots, mine, theirs):
    for block, piece, rows in blocks_of(meta, pieces, slots):
        out = lax.dot_general(
            piece[rows, :], dec_rows(meta, dec, block), (((1,), (1,)), ((), ())), preferred_element_type=F32
        ).astype(BF)
        mine[rows_of(block), :] = out[:, :LB]
        theirs[rows_of(block), :] = out[:, LB:]


def near_dcodes_kernel(meta, dec, *refs):
    pieces = list(refs[:7]) + [None] * 2 + list(refs[7:14]) + [None] * 2
    dcodes_of(meta, dec, pieces, range(7), *refs[14:])


def all_dcodes_kernel(meta, dec, near_mine, near_theirs, *refs):
    mine, theirs = refs[-2:]
    mine[...] = near_mine[...]
    theirs[...] = near_theirs[...]
    pieces = [None] * 7 + list(refs[:2]) + [None] * 7 + list(refs[2:4])
    dcodes_of(meta, dec, pieces, (7, 8), mine, theirs)


def make_dcodes(meta, dec, pieces):
    out = shape(NTB * TB, LB)
    near = [p for c in range(CHAINS) for p in pieces[c * NP : c * NP + 7]]
    far = [p for c in range(CHAINS) for p in pieces[c * NP + 7 : c * NP + 9]]
    flops = MATMUL * dec.shape[1]
    first = call(
        near_dcodes_kernel, "near_dcodes", [SMEM] + [VMEM] * (1 + len(near)), [out, out], (meta, dec, *near), flops
    )
    return call(
        all_dcodes_kernel, "all_dcodes", [SMEM] + [VMEM] * (3 + len(far)), [out, out], (meta, dec, *first, *far), flops // 8
    )


def accumulate(meta, both, right, acc):
    def body(b, carry):
        ia, ib = pair_of(meta, b)
        prod = lax.dot_general(
            both[rows_of(b), :], right[rows_of(b), :], (((0,), (0,)), ((), ())), preferred_element_type=F32
        )
        acc[rows_of(ia), :] += prod[:LB]
        acc[rows_of(ib), :] += prod[LB:]
        return carry

    acc[...] = jnp.zeros_like(acc)
    lax.fori_loop(0, NTB, body, 0, unroll=8)


def dec_grad_kernel(meta, both, *refs):
    pieces, (out, done, delta, acc) = refs[:-4], refs[-4:]
    for block, piece, rows in blocks_of(meta, pieces):
        delta[rows_of(block), :] = piece[rows, :]
    accumulate(meta, both, delta, acc)
    out[...] = acc[...].astype(BF)
    done[...] = delta[: done.shape[0], : done.shape[1]]


def make_dec_grad(meta, like, both, pieces):
    return call(
        dec_grad_kernel,
        "dec_grad",
        [SMEM] + [VMEM] * (1 + len(pieces)),
        [shape(*like.shape), shape(16, LB)],
        (meta, both, *pieces),
        MATMUL * like.shape[1],
        [pltpu.VMEM((NTB * TB, like.shape[1]), BF), pltpu.VMEM(like.shape, F32)],
    )


def enc_grad_kernel(meta, cap, *refs):
    out, both, acc = refs[2 * SIDE :]
    join_slots(meta, refs[:SIDE], refs[SIDE : 2 * SIDE], both)
    accumulate(meta, both, cap, acc)
    for i in range(acc.shape[0] // LB):
        tile = slice(i * LB, (i + 1) * LB)
        out[:, tile] = acc[tile, :].T.astype(BF)


def make_enc_grad(meta, captured, like, mine, other):
    return call(
        enc_grad_kernel,
        "enc_grad",
        [SMEM] + [VMEM] * (1 + 2 * SIDE),
        shape(*like.shape),
        (meta, captured, *mine, *other),
        MATMUL * like.shape[0],
        [pltpu.VMEM((NTB * TB, KS * LB), BF), pltpu.VMEM(like.shape[::-1], F32)],
    )


def local(captured, enc_weight, enc_bias, dec_weight, dec_bias, block_ids, block_counts):
    y, x, core = (lax.axis_index(a) for a in ("y", "x", "core"))
    first, second = jnp.where(core == 0, x, y), jnp.where(core == 0, y, x)
    place = jnp.stack([core, first, second, lax.axis_index("lat")]).astype(jnp.int32)
    meta = jnp.concatenate([block_ids.reshape(-1), block_counts.reshape(-1), place])

    terms = tok_scatter(meta, *encode(meta, captured, enc_weight))
    codes = call(
        codes_kernel,
        "codes",
        [SMEM] + [VMEM] * (SIDE + 1),
        shape(*terms[0].shape),
        (meta, *terms, enc_bias.reshape(-1, LB)),
        20 * terms[0].size,
    )
    both, chains = make_parts(meta, *tok_gather(codes), dec_weight)
    pieces = gather_z(reduce_z(meta, chains, dec_bias.reshape(1, -1), captured))
    dec_grad, done = make_dec_grad(meta, dec_weight, both, pieces)
    terms = tok_scatter(meta, *make_dcodes(meta, dec_weight, pieces), beside=(done,))
    dpre = call(
        dpre_kernel, "dpre", [VMEM] * (SIDE + 1), shape(*codes.shape), (*terms, codes), 20 * codes.size
    )
    enc_grad = make_enc_grad(meta, captured, enc_weight, *tok_gather(dpre))
    return enc_grad, dec_grad


def solution(mesh):
    cube = Mesh(mesh.devices.reshape(NY, NX, NC, NZ), ("y", "x", "core", "lat"))
    tok = ("y", "x", "core")
    in_specs = (
        P(None, tok),
        P(tok, "lat"),
        P("lat"),
        P("lat", tok),
        P(tok),
        P(None, "lat", None),
        P(None, "lat"),
    )
    out_specs = (P(tok, "lat"), P("lat", tok))
    return jax.shard_map(local, mesh=cube, in_specs=in_specs, out_specs=out_specs, check_vma=False)
```

```python
import functools

import jax
import jax.numpy as jnp
from jax import lax
from jax.experimental import pallas as pl
from jax.experimental.pallas import tpu as pltpu
from jax.sharding import Mesh, PartitionSpec as P

TB = 128
LB = 128
KS = 2
NTB = 32
NY, NX, NC, NZ = 4, 4, 2, 8
SIDE = 4
CHAINS = 2
QB = NTB // SIDE
ZB = NTB // NZ // CHAINS
FULL = ZB * TB
HALF = FULL // 2

SCALE_ERR = 0.0625
PENALTY = 0.05

BF = jnp.bfloat16
F32 = jnp.float32
VMEM_LIMIT = 24 * 1024 * 1024
ENCODE_LIMIT = 60 * 1024 * 1024

COUNTS = NTB * KS
CORE, FIRST, SECOND, ZPOS = (COUNTS + NTB + i for i in range(4))

SMEM = pl.BlockSpec(memory_space=pltpu.SMEM)
VMEM = pl.BlockSpec(memory_space=pltpu.VMEM)
HBM = pl.BlockSpec(memory_space=pltpu.HBM)


def cost(flops, nbytes):
    return pl.CostEstimate(flops=flops, bytes_accessed=nbytes, transcendentals=0)


def call(kernel, name, in_specs, out_shape, args, flops, scratch=(), aliases=None, limit=VMEM_LIMIT):
    outs = out_shape if isinstance(out_shape, list) else [out_shape]
    nbytes = sum(a.size * a.dtype.itemsize for a in (*args, *outs))
    return pl.pallas_call(
        kernel,
        in_specs=in_specs,
        out_specs=[VMEM] * len(out_shape) if isinstance(out_shape, list) else VMEM,
        out_shape=out_shape,
        scratch_shapes=list(scratch),
        input_output_aliases=aliases or {},
        compiler_params=pltpu.CompilerParams(vmem_limit_bytes=limit),
        cost_estimate=cost(flops, nbytes),
        name=name,
    )(*args)


def shape(*dims, dtype=BF):
    return jax.ShapeDtypeStruct(dims, dtype)


def rows_of(block, count=1):
    return pl.ds(pl.multiple_of(block * TB, TB), count * TB)


def pair_of(meta, block):
    core = meta[CORE]
    return meta[KS * block + core], meta[KS * block + 1 - core]


def ring4(place, step):
    return lax.rem(place + step + SIDE, SIDE)


def total(refs, rows=slice(None)):
    out = refs[0][rows, :].astype(F32)
    for ref in refs[1:]:
        out += ref[rows, :].astype(F32)
    return out


MATMUL = 2 * NTB * TB * KS * LB


def enc_kernel(ids, place, cap_hbm, enc_hbm, mine, theirs, cap, enc, sems):
    tiles, n = enc.shape[0], SIDE
    rows = cap.shape[0] // n
    loads = [pltpu.make_async_copy(enc_hbm.at[:, pl.ds(i * LB, LB)], enc.at[i], sems.at[i]) for i in range(tiles)]
    caps = [
        pltpu.make_async_copy(cap_hbm.at[pl.ds(i * rows, rows)], cap.at[pl.ds(i * rows, rows)], sems.at[tiles + i])
        for i in range(n)
    ]
    for copy in loads + caps:
        copy.start()
    for copy in loads:
        copy.wait()
    core = place[0]

    def body(b, carry):
        w = jnp.concatenate([enc[ids[b, core]], enc[ids[b, 1 - core]]], axis=1)
        out = jnp.dot(cap[rows_of(b), :], w, preferred_element_type=F32).astype(BF)
        mine[rows_of(b), :] = out[:, :LB]
        theirs[rows_of(b), :] = out[:, LB:]
        return carry

    for i in range(n):
        caps[i].wait()
        lax.fori_loop(i * (NTB // n), (i + 1) * (NTB // n), body, 0, unroll=8)


def encode(ids, place, captured, enc):
    out = shape(NTB * TB, LB)
    tiles = enc.shape[1] // LB
    return call(
        enc_kernel,
        "encode",
        [SMEM, SMEM, HBM, HBM],
        [out, out],
        (ids, place, captured, enc),
        MATMUL * enc.shape[0],
        [
            pltpu.VMEM(captured.shape, BF),
            pltpu.VMEM((tiles, enc.shape[0], LB), BF),
            pltpu.SemaphoreType.DMA((tiles + SIDE,)),
        ],
        limit=ENCODE_LIMIT,
    )


def split_add_kernel(meta, mine, got, *quarters):
    for k in range(SIDE):
        quarters[k][...] = total((mine, got), rows_of(ring4(meta[FIRST], k) * QB, QB)).astype(BF)


def total4(refs, rows=slice(None)):
    return total(refs[:2], rows) + total(refs[2:4], rows)


def quarter_sum_kernel(*refs):
    refs[SIDE][...] = total4(refs).astype(BF)


SWAP = [(0, 1), (1, 0)]


def swap(x):
    return lax.ppermute(x, "core", SWAP)


def tok_perm(first, step):
    pairs = []
    for y in range(NY):
        for x in range(NX):
            for c in range(NC):
                ty, tx = (y, (x + step) % NX) if (c == 0) == first else ((y + step) % NY, x)
                pairs.append(((y * NX + x) * NC + c, (ty * NX + tx) * NC + c))
    return pairs


def send(x, first, step):
    return lax.ppermute(x, ("y", "x", "core"), tok_perm(first, step))


def exchange(pieces, first):
    return [pieces[0]] + [send(pieces[k], first, k) for k in (2, 1, 3)]


def copy_kernel(x, out):
    out[...] = x[...]


def tok_scatter(meta, mine, theirs, beside=(), stage=False):
    got = swap(theirs)
    mine = call(copy_kernel, "stage", [VMEM], shape(*mine.shape), (mine,), 0) if stage else mine
    quarters = call(
        split_add_kernel, "split_add", [SMEM, VMEM, VMEM], [shape(QB * TB, LB)] * SIDE, (meta, mine, got), mine.size
    )
    terms = exchange(quarters, True)
    quarter = call(
        lambda *refs: quarter_sum_kernel(*refs[:SIDE], refs[-1]),
        "quarter_sum",
        [VMEM] * SIDE + [VMEM] * len(beside),
        shape(QB * TB, LB),
        (*terms, *beside),
        mine.size,
    )
    return exchange([quarter] * SIDE, False)


def tok_gather(own):
    mine = [own] + [send(own, True, k) for k in range(1, SIDE)]
    return mine, [swap(q) for q in mine]


def join_slots(meta, mine, other, both):
    for k in range(SIDE):
        both[rows_of(ring4(meta[FIRST], -k) * QB, QB), :LB] = mine[k][...]
        both[rows_of(ring4(meta[SECOND], -k) * QB, QB), LB:] = other[k][...]


def codes_kernel(meta, *refs):
    terms, (bias, own) = refs[:SIDE], refs[SIDE:]
    core = meta[CORE]
    for q in range(QB):
        block = meta[FIRST] * QB + q
        rows = slice(q * TB, (q + 1) * TB)
        v = total4(terms, rows) + bias[pl.ds(meta[KS * block + core], 1), :]
        soft = jnp.maximum(v, 0.0) + jnp.log1p(jnp.exp(-jnp.abs(v)))
        own[rows, :] = jnp.where(core < meta[COUNTS + block], soft, 0.0).astype(BF)


def dpre_kernel(*refs):
    terms, (own, out) = refs[:SIDE], refs[SIDE:]
    grads = (total4(terms) + PENALTY) * (1.0 - jnp.exp(-own[...].astype(F32)))
    for i in range(QB):
        tile = slice(i * TB, (i + 1) * TB)
        out[tile, :] = grads[tile, :].T.astype(BF)


ORDER = (0, 1, 7, 2, 6, 3, 5, 4, 4)
NP = len(ORDER)


def piece_shapes(feats):
    return [shape(FULL, feats)] * 7 + [shape(HALF, feats)] * 2


def blocks_of(meta, pieces, slots=range(NP)):
    for slot in slots:
        chunk = lax.rem(meta[ZPOS] + ORDER[slot], NZ)
        for chain in range(CHAINS):
            ref = pieces[chain * NP + slot]
            base = chunk * ZB * CHAINS + chain * ZB + (ZB // 2 if slot == 8 else 0)
            for j in range(ref.shape[0] // TB):
                yield base + j, ref, slice(j * TB, (j + 1) * TB)


def dec_rows(meta, dec, block):
    ia, ib = pair_of(meta, block)
    return jnp.concatenate([dec[rows_of(ia), :], dec[rows_of(ib), :]], axis=0)


def parts_of(meta, dec, both, pieces, slots):
    for block, piece, rows in blocks_of(meta, pieces, slots):
        out = jnp.dot(both[rows_of(block), :], dec_rows(meta, dec, block), preferred_element_type=F32)
        piece[rows, :] = out.astype(BF)


def far_parts_kernel(meta, dec, *refs):
    both, pieces = refs[2 * SIDE], refs[2 * SIDE + 1 :]
    join_slots(meta, refs[:SIDE], refs[SIDE : 2 * SIDE], both)
    pieces = [None] * 7 + list(pieces[:2]) + [None] * 7 + list(pieces[2:])
    parts_of(meta, dec, both, pieces, (7, 8))


def near_parts_kernel(meta, dec, both, *pieces):
    pieces = list(pieces[:7]) + [None] * 2 + list(pieces[7:]) + [None] * 2
    parts_of(meta, dec, both, pieces, (5, 6, 3, 4, 1, 2, 0))


def make_parts(meta, mine, other, dec):
    feats = dec.shape[1]
    shapes = piece_shapes(feats)
    both, *far = call(
        far_parts_kernel,
        "far_parts",
        [SMEM] + [VMEM] * (1 + 2 * SIDE),
        [shape(NTB * TB, KS * LB)] + shapes[7:] * CHAINS,
        (meta, dec, *mine, *other),
        MATMUL * feats // 8,
    )
    near = call(
        near_parts_kernel,
        "near_parts",
        [SMEM] + [VMEM] * 2,
        shapes[:7] * CHAINS,
        (meta, dec, both),
        MATMUL * feats,
    )
    return both, [[*near[c * 7 : c * 7 + 7], *far[c * 2 : c * 2 + 2]] for c in range(CHAINS)]


def add_kernel(pa, ra, pb, rb, oa, ob):
    oa[...] = total((pa, ra)).astype(BF)
    ob[...] = total((pb, rb)).astype(BF)


def add_first_kernel(pa, ra, pb, rb, oa, ob):
    oa[:HALF, :] = (pa[:HALF, :].astype(F32) + ra[...].astype(F32)).astype(BF)
    oa[HALF:, :] = pa[HALF:, :]
    ob[:HALF, :] = pb[:HALF, :]
    ob[HALF:, :] = (pb[HALF:, :].astype(F32) + rb[...].astype(F32)).astype(BF)


def add_both(kernel, *args):
    return call(kernel, "ring_add", [VMEM] * 4, [shape(*args[0].shape)] * 2, args, args[0].size)


def delta_kernel(chain, meta, part, ra, rb, bias, cap, out):
    rows = rows_of((meta[ZPOS] * CHAINS + chain) * ZB, ZB)
    rec = total((part, ra, rb))
    out[...] = (SCALE_ERR * (rec + bias[...] - cap[rows, :].astype(F32))).astype(BF)


RIGHT = [(i, (i + 1) % NZ) for i in range(NZ)]
LEFT = [(i, (i - 1) % NZ) for i in range(NZ)]


def to_right(x):
    return lax.ppermute(x, "lat", RIGHT)


def to_left(x):
    return lax.ppermute(x, "lat", LEFT)


def reduce_z(meta, chains, bias, captured):
    moving = [(to_right(p[7]), to_left(p[8])) for p in chains]
    for slot in (5, 3, 1):
        kernel = add_first_kernel if slot == 5 else add_kernel
        sums = [add_both(kernel, p[slot], r, p[slot + 1], l) for p, (r, l) in zip(chains, moving)]
        moving = [(to_right(a), to_left(b)) for a, b in sums]
    return [
        call(
            functools.partial(delta_kernel, c),
            "delta",
            [SMEM] + [VMEM] * 5,
            shape(*p[0].shape),
            (meta, p[0], r, l, bias, captured),
            6 * p[0].size,
        )
        for c, (p, (r, l)) in enumerate(zip(chains, moving))
    ]


def gather_z(deltas):
    out = [[own] for own in deltas]
    moving = [(own, own) for own in deltas]
    for _ in range(3):
        moving = [(to_right(r), to_left(l)) for r, l in moving]
        for pieces, (r, l) in zip(out, moving):
            pieces += [l, r]
    for pieces, (r, l) in zip(out, moving):
        pieces += [to_right(r[:HALF]), to_left(l[HALF:])]
    return [piece for pieces in out for piece in pieces]


def dcodes_of(meta, dec, pieces, slots, mine, theirs):
    for block, piece, rows in blocks_of(meta, pieces, slots):
        out = lax.dot_general(
            piece[rows, :], dec_rows(meta, dec, block), (((1,), (1,)), ((), ())), preferred_element_type=F32
        ).astype(BF)
        mine[rows_of(block), :] = out[:, :LB]
        theirs[rows_of(block), :] = out[:, LB:]


def near_dcodes_kernel(meta, dec, *refs):
    pieces = list(refs[:7]) + [None] * 2 + list(refs[7:14]) + [None] * 2
    dcodes_of(meta, dec, pieces, range(7), *refs[14:])


def all_dcodes_kernel(meta, dec, near_mine, near_theirs, *refs):
    mine, theirs = refs[-2:]
    mine[...] = near_mine[...]
    theirs[...] = near_theirs[...]
    pieces = [None] * 7 + list(refs[:2]) + [None] * 7 + list(refs[2:4])
    dcodes_of(meta, dec, pieces, (7, 8), mine, theirs)


def make_dcodes(meta, dec, pieces):
    out = shape(NTB * TB, LB)
    near = [p for c in range(CHAINS) for p in pieces[c * NP : c * NP + 7]]
    far = [p for c in range(CHAINS) for p in pieces[c * NP + 7 : c * NP + 9]]
    flops = MATMUL * dec.shape[1]
    first = call(
        near_dcodes_kernel, "near_dcodes", [SMEM] + [VMEM] * (1 + len(near)), [out, out], (meta, dec, *near), flops
    )
    return call(
        all_dcodes_kernel, "all_dcodes", [SMEM] + [VMEM] * (3 + len(far)), [out, out], (meta, dec, *first, *far), flops // 8
    )


def accumulate(meta, both, right, acc):
    def body(b, carry):
        ia, ib = pair_of(meta, b)
        prod = lax.dot_general(
            both[rows_of(b), :], right[rows_of(b), :], (((0,), (0,)), ((), ())), preferred_element_type=F32
        )
        acc[rows_of(ia), :] += prod[:LB]
        acc[rows_of(ib), :] += prod[LB:]
        return carry

    acc[...] = jnp.zeros_like(acc)
    lax.fori_loop(0, NTB, body, 0, unroll=8)


def dec_grad_kernel(meta, both, *refs):
    pieces, (out, done, delta, acc) = refs[:-4], refs[-4:]
    for block, piece, rows in blocks_of(meta, pieces):
        delta[rows_of(block), :] = piece[rows, :]
    accumulate(meta, both, delta, acc)
    out[...] = acc[...].astype(BF)
    done[...] = delta[: done.shape[0], : done.shape[1]]


def make_dec_grad(meta, like, both, pieces):
    return call(
        dec_grad_kernel,
        "dec_grad",
        [SMEM] + [VMEM] * (1 + len(pieces)),
        [shape(*like.shape), shape(16, LB)],
        (meta, both, *pieces),
        MATMUL * like.shape[1],
        [pltpu.VMEM((NTB * TB, like.shape[1]), BF), pltpu.VMEM(like.shape, F32)],
    )


def enc_grad_kernel(meta, cap, *refs):
    out, both, acc = refs[2 * SIDE :]
    for slot, (quarters, at) in enumerate(((refs[:SIDE], FIRST), (refs[SIDE : 2 * SIDE], SECOND))):
        for k in range(SIDE):
            for i in range(QB):
                row = ((ring4(meta[at], -k) * QB + i) * KS + slot)
                both[rows_of(row), :] = quarters[k][i * LB : (i + 1) * LB, :]

    def body(b, carry):
        ia, ib = pair_of(meta, b)
        prod = jnp.dot(both[rows_of(b * KS, KS), :], cap[rows_of(b), :], preferred_element_type=F32)
        acc[rows_of(ia), :] += prod[:LB]
        acc[rows_of(ib), :] += prod[LB:]
        return carry

    acc[...] = jnp.zeros_like(acc)
    lax.fori_loop(0, NTB, body, 0, unroll=8)
    for i in range(acc.shape[0] // LB):
        tile = slice(i * LB, (i + 1) * LB)
        out[:, tile] = acc[tile, :].T.astype(BF)


def make_enc_grad(meta, captured, like, mine, other):
    return call(
        enc_grad_kernel,
        "enc_grad",
        [SMEM] + [VMEM] * (1 + 2 * SIDE),
        shape(*like.shape),
        (meta, captured, *mine, *other),
        MATMUL * like.shape[0],
        [pltpu.VMEM((NTB * KS * LB, TB), BF), pltpu.VMEM(like.shape[::-1], F32)],
    )


def local(captured, enc_weight, enc_bias, dec_weight, dec_bias, block_ids, block_counts):
    y, x, core = (lax.axis_index(a) for a in ("y", "x", "core"))
    first, second = jnp.where(core == 0, x, y), jnp.where(core == 0, y, x)
    place = jnp.stack([core, first, second, lax.axis_index("lat")]).astype(jnp.int32)
    meta = jnp.concatenate([block_ids.reshape(-1), block_counts.reshape(-1), place])

    mine, theirs = encode(block_ids.reshape(-1, KS), place[:1], captured, enc_weight)
    terms = tok_scatter(meta, mine, theirs, stage=True)
    codes = call(
        codes_kernel,
        "codes",
        [SMEM] + [VMEM] * (SIDE + 1),
        shape(*terms[0].shape),
        (meta, *terms, enc_bias.reshape(-1, LB)),
        20 * terms[0].size,
    )
    both, chains = make_parts(meta, *tok_gather(codes), dec_weight)
    pieces = gather_z(reduce_z(meta, chains, dec_bias.reshape(1, -1), captured))
    dec_grad, done = make_dec_grad(meta, dec_weight, both, pieces)
    terms = tok_scatter(meta, *make_dcodes(meta, dec_weight, pieces), beside=(done,))
    dpre = call(
        dpre_kernel, "dpre", [VMEM] * (SIDE + 1), shape(*codes.shape), (*terms, codes), 20 * codes.size
    )
    enc_grad = make_enc_grad(meta, captured, enc_weight, *tok_gather(dpre))
    return enc_grad, dec_grad


def solution(mesh):
    cube = Mesh(mesh.devices.reshape(NY, NX, NC, NZ), ("y", "x", "core", "lat"))
    tok = ("y", "x", "core")
    in_specs = (
        P(None, tok),
        P(tok, "lat"),
        P("lat"),
        P("lat", tok),
        P(tok),
        P(None, "lat", None),
        P(None, "lat"),
    )
    out_specs = (P(tok, "lat"), P("lat", tok))
    return jax.shard_map(local, mesh=cube, in_specs=in_specs, out_specs=out_specs, check_vma=False)
```

```python
import functools

import jax
import jax.numpy as jnp
from jax import lax
from jax.experimental import pallas as pl
from jax.experimental.pallas import tpu as pltpu
from jax.sharding import Mesh, PartitionSpec as P

TB = 128
LB = 128
KS = 2
NTB = 32
NY, NX, NC, NZ = 4, 4, 2, 8
SIDE = 4
CHAINS = 2
QB = NTB // SIDE
ZB = NTB // NZ // CHAINS
FULL = ZB * TB
HALF = FULL // 2

SCALE_ERR = 0.0625
PENALTY = 0.05

BF = jnp.bfloat16
F32 = jnp.float32
VMEM_LIMIT = 24 * 1024 * 1024
ENCODE_LIMIT = 60 * 1024 * 1024

COUNTS = NTB * KS
CORE, FIRST, SECOND, ZPOS = (COUNTS + NTB + i for i in range(4))

SMEM = pl.BlockSpec(memory_space=pltpu.SMEM)
VMEM = pl.BlockSpec(memory_space=pltpu.VMEM)
HBM = pl.BlockSpec(memory_space=pltpu.HBM)


def cost(flops, nbytes):
    return pl.CostEstimate(flops=flops, bytes_accessed=nbytes, transcendentals=0)


def call(kernel, name, in_specs, out_shape, args, flops, scratch=(), aliases=None, limit=VMEM_LIMIT):
    outs = out_shape if isinstance(out_shape, list) else [out_shape]
    nbytes = sum(a.size * a.dtype.itemsize for a in (*args, *outs))
    return pl.pallas_call(
        kernel,
        in_specs=in_specs,
        out_specs=[VMEM] * len(out_shape) if isinstance(out_shape, list) else VMEM,
        out_shape=out_shape,
        scratch_shapes=list(scratch),
        input_output_aliases=aliases or {},
        compiler_params=pltpu.CompilerParams(vmem_limit_bytes=limit),
        cost_estimate=cost(flops, nbytes),
        name=name,
    )(*args)


def shape(*dims, dtype=BF):
    return jax.ShapeDtypeStruct(dims, dtype)


def rows_of(block, count=1):
    return pl.ds(pl.multiple_of(block * TB, TB), count * TB)


def pair_of(meta, block):
    core = meta[CORE]
    return meta[KS * block + core], meta[KS * block + 1 - core]


def ring4(place, step):
    return lax.rem(place + step + SIDE, SIDE)


def sent_at(block, place):
    return lax.rem(block // QB + 2 * SIDE - 1 - place, SIDE) * QB + lax.rem(block, QB)


def total(refs, rows=slice(None)):
    out = refs[0][rows, :].astype(F32)
    for ref in refs[1:]:
        out += ref[rows, :].astype(F32)
    return out


MATMUL = 2 * NTB * TB * KS * LB


def to_halves(outs, mine, theirs):
    half = outs[0].shape[0]
    for i, ref in enumerate((mine, theirs)):
        outs[2 * i][...] = ref[:half, :]
        outs[2 * i + 1][...] = ref[half:, :]


def enc_kernel(ids, place, cap_hbm, enc_hbm, *refs):
    outs, (mine, theirs, cap, enc, sems) = refs[:4], refs[4:]
    tiles, n = enc.shape[0], SIDE
    rows = cap.shape[0] // n
    loads = [pltpu.make_async_copy(enc_hbm.at[:, pl.ds(i * LB, LB)], enc.at[i], sems.at[i]) for i in range(tiles)]
    caps = [
        pltpu.make_async_copy(cap_hbm.at[pl.ds(i * rows, rows)], cap.at[pl.ds(i * rows, rows)], sems.at[tiles + i])
        for i in range(n)
    ]
    for copy in loads + caps:
        copy.start()
    for copy in loads:
        copy.wait()
    core, first, second = place[0], place[1], place[2]

    def body(b, carry):
        w = jnp.concatenate([enc[ids[core, b]], enc[ids[1 - core, b]]], axis=1)
        out = jnp.dot(cap[rows_of(b), :], w, preferred_element_type=F32).astype(BF)
        mine[rows_of(sent_at(b, first)), :] = out[:, :LB]
        theirs[rows_of(sent_at(b, second)), :] = out[:, LB:]
        return carry

    for i in range(n):
        caps[i].wait()
        lax.fori_loop(i * (NTB // n), (i + 1) * (NTB // n), body, 0, unroll=8)
    to_halves(outs, mine, theirs)


def encode(ids, place, captured, enc):
    tiles = enc.shape[1] // LB
    return call(
        enc_kernel,
        "encode",
        [SMEM, SMEM, HBM, HBM],
        [shape(NTB // 2 * TB, LB)] * 4,
        (ids, place, captured, enc),
        MATMUL * enc.shape[0],
        [
            pltpu.VMEM((NTB * TB, LB), BF),
            pltpu.VMEM((NTB * TB, LB), BF),
            pltpu.VMEM(captured.shape, BF),
            pltpu.VMEM((tiles, enc.shape[0], LB), BF),
            pltpu.SemaphoreType.DMA((tiles + SIDE,)),
        ],
        limit=ENCODE_LIMIT,
    )


def split_add_kernel(mine, got, *quarters):
    for k in range(2):
        quarters[k][...] = total((mine, got), slice(k * QB * TB, (k + 1) * QB * TB)).astype(BF)


def total4(refs, rows=slice(None)):
    return total(refs[:2], rows) + total(refs[2:4], rows)


def quarter_sum_kernel(*refs):
    out = total4(refs[:SIDE]).astype(BF)
    for ref in refs[-SIDE:]:
        ref[...] = out


SWAP = [(0, 1), (1, 0)]


def swap(x):
    return lax.ppermute(x, "core", SWAP)


def tok_perm(first, step):
    pairs = []
    for y in range(NY):
        for x in range(NX):
            for c in range(NC):
                ty, tx = (y, (x + step) % NX) if (c == 0) == first else ((y + step) % NY, x)
                pairs.append(((y * NX + x) * NC + c, (ty * NX + tx) * NC + c))
    return pairs


def send(x, first, step):
    return lax.ppermute(x, ("y", "x", "core"), tok_perm(first, step))


def copy_kernel(xa, xb, oa, ob):
    oa[...] = xa[...]
    ob[...] = xb[...]


def tok_scatter(mine, theirs, beside=(), stage=False):
    got = [swap(t) for t in theirs]
    if stage:
        mine = call(copy_kernel, "stage", [VMEM] * 2, [shape(*m.shape) for m in mine], mine, 0)
    quarters = [
        q
        for m, g in zip(mine, got)
        for q in call(split_add_kernel, "split_add", [VMEM] * 2, [shape(QB * TB, LB)] * 2, (m, g), m.size)
    ]
    terms = [quarters[3]] + [send(quarters[k - 1], True, k) for k in (2, 1, 3)]
    copies = call(
        quarter_sum_kernel,
        "quarter_sum",
        [VMEM] * (SIDE + len(beside)),
        [shape(QB * TB, LB)] * SIDE,
        (*terms, *beside),
        4 * quarters[0].size,
    )
    return [copies[0]] + [send(copies[k], False, k) for k in (2, 1, 3)]


def tok_gather(copies):
    got = {k: send(copies[k], True, k) for k in (2, 1, 3)}
    mine = [copies[0]] + [got[k] for k in range(1, SIDE)]
    return mine, [swap(q) for q in mine]


def join_slots(meta, mine, other, both):
    for k in range(SIDE):
        both[rows_of(ring4(meta[FIRST], -k) * QB, QB), :LB] = mine[k][...]
        both[rows_of(ring4(meta[SECOND], -k) * QB, QB), LB:] = other[k][...]


def codes_kernel(meta, *refs):
    terms, bias, copies = refs[:SIDE], refs[SIDE], refs[SIDE + 1 :]
    core = meta[CORE]
    for q in range(QB):
        block = meta[FIRST] * QB + q
        rows = slice(q * TB, (q + 1) * TB)
        v = total4(terms, rows) + bias[pl.ds(meta[KS * block + core], 1), :]
        soft = jnp.maximum(v, 0.0) + jnp.log1p(jnp.exp(-jnp.abs(v)))
        code = jnp.where(core < meta[COUNTS + block], soft, 0.0).astype(BF)
        for ref in copies:
            ref[rows, :] = code


def dpre_kernel(*refs):
    terms, own, copies = refs[:SIDE], refs[SIDE], refs[SIDE + 1 :]
    grads = (total4(terms) + PENALTY) * (1.0 - jnp.exp(-own[...].astype(F32)))
    for i in range(QB):
        tile = slice(i * TB, (i + 1) * TB)
        turned = grads[tile, :].T.astype(BF)
        for ref in copies:
            ref[tile, :] = turned


ORDER = (0, 1, 7, 2, 6, 3, 5, 4, 4)
NP = len(ORDER)


def piece_shapes(feats):
    return [shape(FULL, feats)] * 7 + [shape(HALF, feats)] * 2


def blocks_of(meta, pieces, slots=range(NP)):
    for slot in slots:
        chunk = lax.rem(meta[ZPOS] + ORDER[slot], NZ)
        for chain in range(CHAINS):
            ref = pieces[chain * NP + slot]
            base = chunk * ZB * CHAINS + chain * ZB + (ZB // 2 if slot == 8 else 0)
            for j in range(ref.shape[0] // TB):
                yield base + j, ref, slice(j * TB, (j + 1) * TB)


def dec_rows(meta, dec, block):
    ia, ib = pair_of(meta, block)
    return jnp.concatenate([dec[rows_of(ia), :], dec[rows_of(ib), :]], axis=0)


def parts_of(meta, dec, both, pieces, slots):
    for block, piece, rows in blocks_of(meta, pieces, slots):
        out = jnp.dot(both[rows_of(block), :], dec_rows(meta, dec, block), preferred_element_type=F32)
        piece[rows, :] = out.astype(BF)


def far_parts_kernel(meta, dec, *refs):
    both, pieces = refs[2 * SIDE], refs[2 * SIDE + 1 :]
    join_slots(meta, refs[:SIDE], refs[SIDE : 2 * SIDE], both)
    pieces = [None] * 7 + list(pieces[:2]) + [None] * 7 + list(pieces[2:])
    parts_of(meta, dec, both, pieces, (7, 8))


def near_parts_kernel(meta, dec, both, *pieces):
    pieces = list(pieces[:7]) + [None] * 2 + list(pieces[7:]) + [None] * 2
    parts_of(meta, dec, both, pieces, (5, 6, 3, 4, 1, 2, 0))


def make_parts(meta, mine, other, dec):
    feats = dec.shape[1]
    shapes = piece_shapes(feats)
    both, *far = call(
        far_parts_kernel,
        "far_parts",
        [SMEM] + [VMEM] * (1 + 2 * SIDE),
        [shape(NTB * TB, KS * LB)] + shapes[7:] * CHAINS,
        (meta, dec, *mine, *other),
        MATMUL * feats // 8,
    )
    near = call(
        near_parts_kernel,
        "near_parts",
        [SMEM] + [VMEM] * 2,
        shapes[:7] * CHAINS,
        (meta, dec, both),
        MATMUL * feats,
    )
    return both, [[*near[c * 7 : c * 7 + 7], *far[c * 2 : c * 2 + 2]] for c in range(CHAINS)]


def add_kernel(pa, ra, pb, rb, oa, ob):
    oa[...] = total((pa, ra)).astype(BF)
    ob[...] = total((pb, rb)).astype(BF)


def add_first_kernel(pa, ra, pb, rb, oa, ob):
    oa[:HALF, :] = (pa[:HALF, :].astype(F32) + ra[...].astype(F32)).astype(BF)
    oa[HALF:, :] = pa[HALF:, :]
    ob[:HALF, :] = pb[:HALF, :]
    ob[HALF:, :] = (pb[HALF:, :].astype(F32) + rb[...].astype(F32)).astype(BF)


def add_both(kernel, *args):
    return call(kernel, "ring_add", [VMEM] * 4, [shape(*args[0].shape)] * 2, args, args[0].size)


def delta_kernel(chain, meta, part, ra, rb, bias, cap, out):
    rows = rows_of((meta[ZPOS] * CHAINS + chain) * ZB, ZB)
    rec = total((part, ra, rb))
    out[...] = (SCALE_ERR * (rec + bias[...] - cap[rows, :].astype(F32))).astype(BF)


RIGHT = [(i, (i + 1) % NZ) for i in range(NZ)]
LEFT = [(i, (i - 1) % NZ) for i in range(NZ)]


def to_right(x):
    return lax.ppermute(x, "lat", RIGHT)


def to_left(x):
    return lax.ppermute(x, "lat", LEFT)


def reduce_z(meta, chains, bias, captured):
    moving = [(to_right(p[7]), to_left(p[8])) for p in chains]
    for slot in (5, 3, 1):
        kernel = add_first_kernel if slot == 5 else add_kernel
        sums = [add_both(kernel, p[slot], r, p[slot + 1], l) for p, (r, l) in zip(chains, moving)]
        moving = [(to_right(a), to_left(b)) for a, b in sums]
    return [
        call(
            functools.partial(delta_kernel, c),
            "delta",
            [SMEM] + [VMEM] * 5,
            shape(*p[0].shape),
            (meta, p[0], r, l, bias, captured),
            6 * p[0].size,
        )
        for c, (p, (r, l)) in enumerate(zip(chains, moving))
    ]


def gather_z(deltas):
    out = [[own] for own in deltas]
    moving = [(own, own) for own in deltas]
    for _ in range(3):
        moving = [(to_right(r), to_left(l)) for r, l in moving]
        for pieces, (r, l) in zip(out, moving):
            pieces += [l, r]
    for pieces, (r, l) in zip(out, moving):
        pieces += [to_right(r[:HALF]), to_left(l[HALF:])]
    return [piece for pieces in out for piece in pieces]


def dcodes_of(meta, dec, pieces, slots, put):
    for block, piece, rows in blocks_of(meta, pieces, slots):
        out = lax.dot_general(
            piece[rows, :], dec_rows(meta, dec, block), (((1,), (1,)), ((), ())), preferred_element_type=F32
        ).astype(BF)
        put(0, sent_at(block, meta[FIRST]), out[:, :LB])
        put(1, sent_at(block, meta[SECOND]), out[:, LB:])


def near_dcodes_kernel(meta, dec, *refs):
    pieces = list(refs[:7]) + [None] * 2 + list(refs[7:14]) + [None] * 2
    outs = refs[14:]

    def put(i, at, value):
        outs[i][rows_of(at), :] = value

    dcodes_of(meta, dec, pieces, range(7), put)


def all_dcodes_kernel(meta, dec, near_mine, near_theirs, *refs):
    outs = refs[-4:]
    to_halves(outs, near_mine, near_theirs)

    def put(i, at, value):
        for half in range(2):

            @pl.when(at // (NTB // 2) == half)
            def _():
                outs[2 * i + half][rows_of(at - half * (NTB // 2)), :] = value

    pieces = [None] * 7 + list(refs[:2]) + [None] * 7 + list(refs[2:4])
    dcodes_of(meta, dec, pieces, (7, 8), put)


def make_dcodes(meta, dec, pieces):
    out = shape(NTB * TB, LB)
    near = [p for c in range(CHAINS) for p in pieces[c * NP : c * NP + 7]]
    far = [p for c in range(CHAINS) for p in pieces[c * NP + 7 : c * NP + 9]]
    flops = MATMUL * dec.shape[1]
    first = call(
        near_dcodes_kernel, "near_dcodes", [SMEM] + [VMEM] * (1 + len(near)), [out, out], (meta, dec, *near), flops
    )
    return call(
        all_dcodes_kernel,
        "all_dcodes",
        [SMEM] + [VMEM] * (3 + len(far)),
        [shape(NTB // 2 * TB, LB)] * 4,
        (meta, dec, *first, *far),
        flops // 8,
    )


def accumulate(meta, both, right, acc):
    def body(b, carry):
        ia, ib = pair_of(meta, b)
        prod = lax.dot_general(
            both[rows_of(b), :], right[rows_of(b), :], (((0,), (0,)), ((), ())), preferred_element_type=F32
        )
        acc[rows_of(ia), :] += prod[:LB]
        acc[rows_of(ib), :] += prod[LB:]
        return carry

    acc[...] = jnp.zeros_like(acc)
    lax.fori_loop(0, NTB, body, 0, unroll=8)


def dec_grad_kernel(meta, both, *refs):
    pieces, (out, done, delta, acc) = refs[:-4], refs[-4:]
    for block, piece, rows in blocks_of(meta, pieces):
        delta[rows_of(block), :] = piece[rows, :]
    accumulate(meta, both, delta, acc)
    out[...] = acc[...].astype(BF)
    done[...] = delta[: done.shape[0], : done.shape[1]]


def make_dec_grad(meta, like, both, pieces):
    return call(
        dec_grad_kernel,
        "dec_grad",
        [SMEM] + [VMEM] * (1 + len(pieces)),
        [shape(*like.shape), shape(16, LB)],
        (meta, both, *pieces),
        MATMUL * like.shape[1],
        [pltpu.VMEM((NTB * TB, like.shape[1]), BF), pltpu.VMEM(like.shape, F32)],
    )


def enc_grad_kernel(meta, cap, *refs):
    out, both, acc = refs[2 * SIDE :]
    for slot, (quarters, at) in enumerate(((refs[:SIDE], FIRST), (refs[SIDE : 2 * SIDE], SECOND))):
        for k in range(SIDE):
            for i in range(QB):
                row = ((ring4(meta[at], -k) * QB + i) * KS + slot)
                both[rows_of(row), :] = quarters[k][i * LB : (i + 1) * LB, :]

    def body(b, carry):
        ia, ib = pair_of(meta, b)
        prod = jnp.dot(both[rows_of(b * KS, KS), :], cap[rows_of(b), :], preferred_element_type=F32)
        acc[rows_of(ia), :] += prod[:LB]
        acc[rows_of(ib), :] += prod[LB:]
        return carry

    acc[...] = jnp.zeros_like(acc)
    lax.fori_loop(0, NTB, body, 0, unroll=8)
    for i in range(acc.shape[0] // LB):
        tile = slice(i * LB, (i + 1) * LB)
        out[:, tile] = acc[tile, :].T.astype(BF)


def make_enc_grad(meta, captured, like, mine, other):
    return call(
        enc_grad_kernel,
        "enc_grad",
        [SMEM] + [VMEM] * (1 + 2 * SIDE),
        shape(*like.shape),
        (meta, captured, *mine, *other),
        MATMUL * like.shape[0],
        [pltpu.VMEM((NTB * KS * LB, TB), BF), pltpu.VMEM(like.shape[::-1], F32)],
    )


def local(captured, enc_weight, enc_bias, dec_weight, dec_bias, block_ids, block_counts):
    y, x, core = (lax.axis_index(a) for a in ("y", "x", "core"))
    first, second = jnp.where(core == 0, x, y), jnp.where(core == 0, y, x)
    place = jnp.stack([core, first, second, lax.axis_index("lat")]).astype(jnp.int32)
    meta = jnp.concatenate([block_ids.reshape(-1), block_counts.reshape(-1), place])

    sums = encode(block_ids.transpose(1, 2, 0).reshape(KS, -1), place, captured, enc_weight)
    terms = tok_scatter(sums[:2], sums[2:], stage=True)
    codes = call(
        codes_kernel,
        "codes",
        [SMEM] + [VMEM] * (SIDE + 1),
        [shape(*terms[0].shape)] * SIDE,
        (meta, *terms, enc_bias.reshape(-1, LB)),
        20 * terms[0].size,
    )
    both, chains = make_parts(meta, *tok_gather(codes), dec_weight)
    pieces = gather_z(reduce_z(meta, chains, dec_bias.reshape(1, -1), captured))
    dec_grad, done = make_dec_grad(meta, dec_weight, both, pieces)
    sums = make_dcodes(meta, dec_weight, pieces)
    terms = tok_scatter(sums[:2], sums[2:], beside=(done,))
    dpre = call(
        dpre_kernel,
        "dpre",
        [VMEM] * (SIDE + 1),
        [shape(*codes[0].shape)] * SIDE,
        (*terms, codes[0]),
        20 * codes[0].size,
    )
    enc_grad = make_enc_grad(meta, captured, enc_weight, *tok_gather(dpre))
    return enc_grad, dec_grad


def solution(mesh):
    cube = Mesh(mesh.devices.reshape(NY, NX, NC, NZ), ("y", "x", "core", "lat"))
    tok = ("y", "x", "core")
    in_specs = (
        P(None, tok),
        P(tok, "lat"),
        P("lat"),
        P("lat", tok),
        P(tok),
        P(None, "lat", None),
        P(None, "lat"),
    )
    out_specs = (P(tok, "lat"), P("lat", tok))
    return jax.shard_map(local, mesh=cube, in_specs=in_specs, out_specs=out_specs, check_vma=False)
```

```python
import functools

import jax
import jax.numpy as jnp
from jax import lax
from jax.experimental import pallas as pl
from jax.experimental.pallas import tpu as pltpu
from jax.sharding import Mesh, PartitionSpec as P

TB = 128
LB = 128
KS = 2
NTB = 32
NY, NX, NC, NZ = 4, 4, 2, 8
SIDE = 4
CHAINS = 2
QB = NTB // SIDE
ZB = NTB // NZ // CHAINS
FULL = ZB * TB
HALF = FULL // 2

SCALE_ERR = 0.0625
PENALTY = 0.05

BF = jnp.bfloat16
F32 = jnp.float32
VMEM_LIMIT = 24 * 1024 * 1024
ENCODE_LIMIT = 60 * 1024 * 1024

COUNTS = NTB * KS
CORE, FIRST, SECOND, ZPOS = (COUNTS + NTB + i for i in range(4))

SMEM = pl.BlockSpec(memory_space=pltpu.SMEM)
VMEM = pl.BlockSpec(memory_space=pltpu.VMEM)
HBM = pl.BlockSpec(memory_space=pltpu.HBM)


def cost(flops, nbytes):
    return pl.CostEstimate(flops=flops, bytes_accessed=nbytes, transcendentals=0)


def call(kernel, name, in_specs, out_shape, args, flops, scratch=(), aliases=None, limit=VMEM_LIMIT):
    outs = out_shape if isinstance(out_shape, list) else [out_shape]
    nbytes = sum(a.size * a.dtype.itemsize for a in (*args, *outs))
    return pl.pallas_call(
        kernel,
        in_specs=in_specs,
        out_specs=[VMEM] * len(out_shape) if isinstance(out_shape, list) else VMEM,
        out_shape=out_shape,
        scratch_shapes=list(scratch),
        input_output_aliases=aliases or {},
        compiler_params=pltpu.CompilerParams(vmem_limit_bytes=limit),
        cost_estimate=cost(flops, nbytes),
        name=name,
    )(*args)


def shape(*dims, dtype=BF):
    return jax.ShapeDtypeStruct(dims, dtype)


def rows_of(block, count=1):
    return pl.ds(pl.multiple_of(block * TB, TB), count * TB)


def pair_of(meta, block):
    core = meta[CORE]
    return meta[KS * block + core], meta[KS * block + 1 - core]


def ring4(place, step):
    return lax.rem(place + step + SIDE, SIDE)


def sent_at(block, place):
    return lax.rem(block // QB + 2 * SIDE - 1 - place, SIDE) * QB + lax.rem(block, QB)


def total(refs, rows=slice(None)):
    out = refs[0][rows, :].astype(F32)
    for ref in refs[1:]:
        out += ref[rows, :].astype(F32)
    return out


MATMUL = 2 * NTB * TB * KS * LB


def to_halves(outs, mine, theirs):
    half = outs[0].shape[0]
    for i, ref in enumerate((mine, theirs)):
        outs[2 * i][...] = ref[:half, :]
        outs[2 * i + 1][...] = ref[half:, :]


def enc_kernel(ids, place, cap_hbm, enc_hbm, *refs):
    outs, (mine, theirs, cap, enc, sems) = refs[:4], refs[4:]
    tiles, n = enc.shape[0], SIDE
    rows = cap.shape[0] // n
    loads = [pltpu.make_async_copy(enc_hbm.at[:, pl.ds(i * LB, LB)], enc.at[i], sems.at[i]) for i in range(tiles)]
    caps = [
        pltpu.make_async_copy(cap_hbm.at[pl.ds(i * rows, rows)], cap.at[pl.ds(i * rows, rows)], sems.at[tiles + i])
        for i in range(n)
    ]
    for copy in loads + caps:
        copy.start()
    for copy in loads:
        copy.wait()
    core, first, second = place[0], place[1], place[2]

    def body(b, carry):
        w = jnp.concatenate([enc[ids[core, b]], enc[ids[1 - core, b]]], axis=1)
        out = jnp.dot(cap[rows_of(b), :], w, preferred_element_type=F32).astype(BF)
        mine[rows_of(sent_at(b, first)), :] = out[:, :LB]
        theirs[rows_of(sent_at(b, second)), :] = out[:, LB:]
        return carry

    for i in range(n):
        caps[i].wait()
        lax.fori_loop(i * (NTB // n), (i + 1) * (NTB // n), body, 0, unroll=8)
    to_halves(outs, mine, theirs)


def encode(ids, place, captured, enc):
    tiles = enc.shape[1] // LB
    return call(
        enc_kernel,
        "encode",
        [SMEM, SMEM, HBM, HBM],
        [shape(NTB // 2 * TB, LB)] * 4,
        (ids, place, captured, enc),
        MATMUL * enc.shape[0],
        [
            pltpu.VMEM((NTB * TB, LB), BF),
            pltpu.VMEM((NTB * TB, LB), BF),
            pltpu.VMEM(captured.shape, BF),
            pltpu.VMEM((tiles, enc.shape[0], LB), BF),
            pltpu.SemaphoreType.DMA((tiles + SIDE,)),
        ],
        limit=ENCODE_LIMIT,
    )


def split_add_kernel(mine, got, *quarters):
    for k in range(len(quarters)):
        quarters[k][...] = total((mine, got), slice(k * QB * TB, (k + 1) * QB * TB)).astype(BF)


def total4(refs, rows=slice(None)):
    return total(refs[:2], rows) + total(refs[2:4], rows)


def quarter_sum_kernel(*refs):
    out = total4(refs[:SIDE]).astype(BF)
    for ref in refs[-SIDE:]:
        ref[...] = out


SWAP = [(0, 1), (1, 0)]


def swap(x):
    return lax.ppermute(x, "core", SWAP)


def tok_perm(first, step):
    pairs = []
    for y in range(NY):
        for x in range(NX):
            for c in range(NC):
                ty, tx = (y, (x + step) % NX) if (c == 0) == first else ((y + step) % NY, x)
                pairs.append(((y * NX + x) * NC + c, (ty * NX + tx) * NC + c))
    return pairs


def send(x, first, step):
    return lax.ppermute(x, ("y", "x", "core"), tok_perm(first, step))


def copy_kernel(xa, xb, oa, ob):
    oa[...] = xa[...]
    ob[...] = xb[...]


def tok_scatter(mine, theirs, beside=(), stage=False):
    got = [swap(t) for t in theirs]
    if stage:
        mine = call(copy_kernel, "stage", [VMEM] * 2, [shape(*m.shape) for m in mine], mine, 0)
    quarters = [
        q
        for m, g in zip(mine, got)
        for q in call(
            split_add_kernel, "split_add", [VMEM] * 2, [shape(QB * TB, LB)] * (SIDE // len(mine)), (m, g), m.size
        )
    ]
    terms = [quarters[3]] + [send(quarters[k - 1], True, k) for k in (2, 1, 3)]
    copies = call(
        quarter_sum_kernel,
        "quarter_sum",
        [VMEM] * (SIDE + len(beside)),
        [shape(QB * TB, LB)] * SIDE,
        (*terms, *beside),
        4 * quarters[0].size,
    )
    return [copies[0]] + [send(copies[k], False, k) for k in (2, 1, 3)]


def tok_gather(copies):
    got = {k: send(copies[k], True, k) for k in (2, 1, 3)}
    mine = [copies[0]] + [got[k] for k in range(1, SIDE)]
    return mine, [swap(q) for q in mine]


def join_slots(meta, mine, other, both):
    for k in range(SIDE):
        both[rows_of(ring4(meta[FIRST], -k) * QB, QB), :LB] = mine[k][...]
        both[rows_of(ring4(meta[SECOND], -k) * QB, QB), LB:] = other[k][...]


def codes_kernel(meta, *refs):
    terms, bias, copies = refs[:SIDE], refs[SIDE], refs[SIDE + 1 :]
    core = meta[CORE]
    for q in range(QB):
        block = meta[FIRST] * QB + q
        rows = slice(q * TB, (q + 1) * TB)
        v = total4(terms, rows) + bias[pl.ds(meta[KS * block + core], 1), :]
        soft = jnp.maximum(v, 0.0) + jnp.log1p(jnp.exp(-jnp.abs(v)))
        code = jnp.where(core < meta[COUNTS + block], soft, 0.0).astype(BF)
        for ref in copies:
            ref[rows, :] = code


def dpre_kernel(*refs):
    terms, own, copies = refs[:SIDE], refs[SIDE], refs[SIDE + 1 :]
    grads = (total4(terms) + PENALTY) * (1.0 - jnp.exp(-own[...].astype(F32)))
    for i in range(QB):
        tile = slice(i * TB, (i + 1) * TB)
        turned = grads[tile, :].T.astype(BF)
        for ref in copies:
            ref[tile, :] = turned


ORDER = (0, 1, 7, 2, 6, 3, 5, 4, 4)
NP = len(ORDER)


def piece_shapes(feats):
    return [shape(FULL, feats)] * 7 + [shape(HALF, feats)] * 2


def blocks_of(meta, pieces, slots=range(NP)):
    for slot in slots:
        chunk = lax.rem(meta[ZPOS] + ORDER[slot], NZ)
        for chain in range(CHAINS):
            ref = pieces[chain * NP + slot]
            base = chunk * ZB * CHAINS + chain * ZB + (ZB // 2 if slot == 8 else 0)
            for j in range(ref.shape[0] // TB):
                yield base + j, ref, slice(j * TB, (j + 1) * TB)


def dec_rows(meta, dec, block):
    ia, ib = pair_of(meta, block)
    return jnp.concatenate([dec[rows_of(ia), :], dec[rows_of(ib), :]], axis=0)


def parts_of(meta, dec, both, pieces, slots):
    for block, piece, rows in blocks_of(meta, pieces, slots):
        out = jnp.dot(both[rows_of(block), :], dec_rows(meta, dec, block), preferred_element_type=F32)
        piece[rows, :] = out.astype(BF)


def far_parts_kernel(meta, dec, *refs):
    both, pieces = refs[2 * SIDE], refs[2 * SIDE + 1 :]
    join_slots(meta, refs[:SIDE], refs[SIDE : 2 * SIDE], both)
    pieces = [None] * 7 + list(pieces[:2]) + [None] * 7 + list(pieces[2:])
    parts_of(meta, dec, both, pieces, (7, 8))


def near_parts_kernel(meta, dec, both, *pieces):
    pieces = list(pieces[:7]) + [None] * 2 + list(pieces[7:]) + [None] * 2
    parts_of(meta, dec, both, pieces, (5, 6, 3, 4, 1, 2, 0))


def make_parts(meta, mine, other, dec):
    feats = dec.shape[1]
    shapes = piece_shapes(feats)
    both, *far = call(
        far_parts_kernel,
        "far_parts",
        [SMEM] + [VMEM] * (1 + 2 * SIDE),
        [shape(NTB * TB, KS * LB)] + shapes[7:] * CHAINS,
        (meta, dec, *mine, *other),
        MATMUL * feats // 8,
    )
    near = call(
        near_parts_kernel,
        "near_parts",
        [SMEM] + [VMEM] * 2,
        shapes[:7] * CHAINS,
        (meta, dec, both),
        MATMUL * feats,
    )
    return both, [[*near[c * 7 : c * 7 + 7], *far[c * 2 : c * 2 + 2]] for c in range(CHAINS)]


def add_kernel(pa, ra, pb, rb, oa, ob):
    oa[...] = total((pa, ra)).astype(BF)
    ob[...] = total((pb, rb)).astype(BF)


def add_first_kernel(pa, ra, pb, rb, oa, ob):
    oa[:HALF, :] = (pa[:HALF, :].astype(F32) + ra[...].astype(F32)).astype(BF)
    oa[HALF:, :] = pa[HALF:, :]
    ob[:HALF, :] = pb[:HALF, :]
    ob[HALF:, :] = (pb[HALF:, :].astype(F32) + rb[...].astype(F32)).astype(BF)


def add_both(kernel, *args):
    return call(kernel, "ring_add", [VMEM] * 4, [shape(*args[0].shape)] * 2, args, args[0].size)


def delta_kernel(chain, meta, part, ra, rb, bias, cap, out):
    rows = rows_of((meta[ZPOS] * CHAINS + chain) * ZB, ZB)
    rec = total((part, ra, rb))
    out[...] = (SCALE_ERR * (rec + bias[...] - cap[rows, :].astype(F32))).astype(BF)


RIGHT = [(i, (i + 1) % NZ) for i in range(NZ)]
LEFT = [(i, (i - 1) % NZ) for i in range(NZ)]


def to_right(x):
    return lax.ppermute(x, "lat", RIGHT)


def to_left(x):
    return lax.ppermute(x, "lat", LEFT)


def reduce_z(meta, chains, bias, captured):
    moving = [(to_right(p[7]), to_left(p[8])) for p in chains]
    for slot in (5, 3, 1):
        kernel = add_first_kernel if slot == 5 else add_kernel
        sums = [add_both(kernel, p[slot], r, p[slot + 1], l) for p, (r, l) in zip(chains, moving)]
        moving = [(to_right(a), to_left(b)) for a, b in sums]
    return [
        call(
            functools.partial(delta_kernel, c),
            "delta",
            [SMEM] + [VMEM] * 5,
            shape(*p[0].shape),
            (meta, p[0], r, l, bias, captured),
            6 * p[0].size,
        )
        for c, (p, (r, l)) in enumerate(zip(chains, moving))
    ]


def gather_z(deltas):
    out = [[own] for own in deltas]
    moving = [(own, own) for own in deltas]
    for _ in range(3):
        moving = [(to_right(r), to_left(l)) for r, l in moving]
        for pieces, (r, l) in zip(out, moving):
            pieces += [l, r]
    for pieces, (r, l) in zip(out, moving):
        pieces += [to_right(r[:HALF]), to_left(l[HALF:])]
    return [piece for pieces in out for piece in pieces]


def dcodes_of(meta, dec, pieces, slots, put):
    for block, piece, rows in blocks_of(meta, pieces, slots):
        out = lax.dot_general(
            piece[rows, :], dec_rows(meta, dec, block), (((1,), (1,)), ((), ())), preferred_element_type=F32
        ).astype(BF)
        put(0, sent_at(block, meta[FIRST]), out[:, :LB])
        put(1, sent_at(block, meta[SECOND]), out[:, LB:])


def near_dcodes_kernel(meta, dec, *refs):
    pieces = list(refs[:7]) + [None] * 2 + list(refs[7:14]) + [None] * 2
    outs = refs[14:]

    def put(i, at, value):
        outs[i][rows_of(at), :] = value

    dcodes_of(meta, dec, pieces, range(7), put)


def all_dcodes_kernel(meta, dec, near_mine, near_theirs, *refs):
    outs = refs[-2:]
    outs[0][...] = near_mine[...]
    outs[1][...] = near_theirs[...]

    def put(i, at, value):
        outs[i][rows_of(at), :] = value

    pieces = [None] * 7 + list(refs[:2]) + [None] * 7 + list(refs[2:4])
    dcodes_of(meta, dec, pieces, (7, 8), put)


def make_dcodes(meta, dec, pieces):
    out = shape(NTB * TB, LB)
    near = [p for c in range(CHAINS) for p in pieces[c * NP : c * NP + 7]]
    far = [p for c in range(CHAINS) for p in pieces[c * NP + 7 : c * NP + 9]]
    flops = MATMUL * dec.shape[1]
    first = call(
        near_dcodes_kernel, "near_dcodes", [SMEM] + [VMEM] * (1 + len(near)), [out, out], (meta, dec, *near), flops
    )
    return call(
        all_dcodes_kernel,
        "all_dcodes",
        [SMEM] + [VMEM] * (3 + len(far)),
        [out, out],
        (meta, dec, *first, *far),
        flops // 8,
    )


def accumulate(meta, both, right, acc):
    def body(b, carry):
        ia, ib = pair_of(meta, b)
        prod = lax.dot_general(
            both[rows_of(b), :], right[rows_of(b), :], (((0,), (0,)), ((), ())), preferred_element_type=F32
        )
        acc[rows_of(ia), :] += prod[:LB]
        acc[rows_of(ib), :] += prod[LB:]
        return carry

    acc[...] = jnp.zeros_like(acc)
    lax.fori_loop(0, NTB, body, 0, unroll=4)


def dec_grad_kernel(meta, both, *refs):
    pieces, (out, done, delta, acc) = refs[:-4], refs[-4:]
    for block, piece, rows in blocks_of(meta, pieces):
        delta[rows_of(block), :] = piece[rows, :]
    accumulate(meta, both, delta, acc)
    out[...] = acc[...].astype(BF)
    done[...] = delta[: done.shape[0], : done.shape[1]]


def make_dec_grad(meta, like, both, pieces):
    return call(
        dec_grad_kernel,
        "dec_grad",
        [SMEM] + [VMEM] * (1 + len(pieces)),
        [shape(*like.shape), shape(16, LB)],
        (meta, both, *pieces),
        MATMUL * like.shape[1],
        [pltpu.VMEM((NTB * TB, like.shape[1]), BF), pltpu.VMEM(like.shape, F32)],
    )


def enc_grad_kernel(meta, cap, *refs):
    out, both, acc = refs[2 * SIDE :]
    for slot, (quarters, at) in enumerate(((refs[:SIDE], FIRST), (refs[SIDE : 2 * SIDE], SECOND))):
        for k in range(SIDE):
            for i in range(QB):
                row = ((ring4(meta[at], -k) * QB + i) * KS + slot)
                both[rows_of(row), :] = quarters[k][i * LB : (i + 1) * LB, :]

    def body(b, carry):
        ia, ib = pair_of(meta, b)
        prod = jnp.dot(both[rows_of(b * KS, KS), :], cap[rows_of(b), :], preferred_element_type=F32)
        acc[rows_of(ia), :] += prod[:LB]
        acc[rows_of(ib), :] += prod[LB:]
        return carry

    acc[...] = jnp.zeros_like(acc)
    lax.fori_loop(0, NTB, body, 0, unroll=8)
    for i in range(acc.shape[0] // LB):
        tile = slice(i * LB, (i + 1) * LB)
        out[:, tile] = acc[tile, :].T.astype(BF)


def make_enc_grad(meta, captured, like, mine, other):
    return call(
        enc_grad_kernel,
        "enc_grad",
        [SMEM] + [VMEM] * (1 + 2 * SIDE),
        shape(*like.shape),
        (meta, captured, *mine, *other),
        MATMUL * like.shape[0],
        [pltpu.VMEM((NTB * KS * LB, TB), BF), pltpu.VMEM(like.shape[::-1], F32)],
    )


def local(captured, enc_weight, enc_bias, dec_weight, dec_bias, block_ids, block_counts):
    y, x, core = (lax.axis_index(a) for a in ("y", "x", "core"))
    first, second = jnp.where(core == 0, x, y), jnp.where(core == 0, y, x)
    place = jnp.stack([core, first, second, lax.axis_index("lat")]).astype(jnp.int32)
    meta = jnp.concatenate([block_ids.reshape(-1), block_counts.reshape(-1), place])

    sums = encode(block_ids.transpose(1, 2, 0).reshape(KS, -1), place, captured, enc_weight)
    terms = tok_scatter(sums[:2], sums[2:], stage=True)
    codes = call(
        codes_kernel,
        "codes",
        [SMEM] + [VMEM] * (SIDE + 1),
        [shape(*terms[0].shape)] * SIDE,
        (meta, *terms, enc_bias.reshape(-1, LB)),
        20 * terms[0].size,
    )
    both, chains = make_parts(meta, *tok_gather(codes), dec_weight)
    pieces = gather_z(reduce_z(meta, chains, dec_bias.reshape(1, -1), captured))
    dec_grad, done = make_dec_grad(meta, dec_weight, both, pieces)
    sums = make_dcodes(meta, dec_weight, pieces)
    terms = tok_scatter(sums[:1], sums[1:], beside=(done,))
    dpre = call(
        dpre_kernel,
        "dpre",
        [VMEM] * (SIDE + 1),
        [shape(*codes[0].shape)] * SIDE,
        (*terms, codes[0]),
        20 * codes[0].size,
    )
    enc_grad = make_enc_grad(meta, captured, enc_weight, *tok_gather(dpre))
    return enc_grad, dec_grad


def solution(mesh):
    cube = Mesh(mesh.devices.reshape(NY, NX, NC, NZ), ("y", "x", "core", "lat"))
    tok = ("y", "x", "core")
    in_specs = (
        P(None, tok),
        P(tok, "lat"),
        P("lat"),
        P("lat", tok),
        P(tok),
        P(None, "lat", None),
        P(None, "lat"),
    )
    out_specs = (P(tok, "lat"), P("lat", tok))
    return jax.shard_map(local, mesh=cube, in_specs=in_specs, out_specs=out_specs, check_vma=False)
```

```python
import functools

import jax
import jax.numpy as jnp
from jax import lax
from jax.experimental import pallas as pl
from jax.experimental.pallas import tpu as pltpu
from jax.sharding import Mesh, PartitionSpec as P

TB = 128
LB = 128
KS = 2
NTB = 32
NY, NX, NC, NZ = 4, 4, 2, 8
SIDE = 4
CHAINS = 2
QB = NTB // SIDE
ZB = NTB // NZ // CHAINS
FULL = ZB * TB
HALF = FULL // 2

SCALE_ERR = 0.0625
PENALTY = 0.05

BF = jnp.bfloat16
F32 = jnp.float32
VMEM_LIMIT = 24 * 1024 * 1024
ENCODE_LIMIT = 60 * 1024 * 1024

COUNTS = NTB * KS
CORE, FIRST, SECOND, ZPOS = (COUNTS + NTB + i for i in range(4))

SMEM = pl.BlockSpec(memory_space=pltpu.SMEM)
VMEM = pl.BlockSpec(memory_space=pltpu.VMEM)
HBM = pl.BlockSpec(memory_space=pltpu.HBM)


def cost(flops, nbytes):
    return pl.CostEstimate(flops=flops, bytes_accessed=nbytes, transcendentals=0)


def call(kernel, name, in_specs, out_shape, args, flops, scratch=(), aliases=None, limit=VMEM_LIMIT):
    outs = out_shape if isinstance(out_shape, list) else [out_shape]
    nbytes = sum(a.size * a.dtype.itemsize for a in (*args, *outs))
    return pl.pallas_call(
        kernel,
        in_specs=in_specs,
        out_specs=[VMEM] * len(out_shape) if isinstance(out_shape, list) else VMEM,
        out_shape=out_shape,
        scratch_shapes=list(scratch),
        input_output_aliases=aliases or {},
        compiler_params=pltpu.CompilerParams(vmem_limit_bytes=limit),
        cost_estimate=cost(flops, nbytes),
        name=name,
    )(*args)


def shape(*dims, dtype=BF):
    return jax.ShapeDtypeStruct(dims, dtype)


def rows_of(block, count=1):
    return pl.ds(pl.multiple_of(block * TB, TB), count * TB)


def pair_of(meta, block):
    core = meta[CORE]
    return meta[KS * block + core], meta[KS * block + 1 - core]


def ring4(place, step):
    return lax.rem(place + step + SIDE, SIDE)


def sent_at(block, place):
    return lax.rem(block // QB + 2 * SIDE - 1 - place, SIDE) * QB + lax.rem(block, QB)


def total(refs, rows=slice(None)):
    out = refs[0][rows, :].astype(F32)
    for ref in refs[1:]:
        out += ref[rows, :].astype(F32)
    return out


MATMUL = 2 * NTB * TB * KS * LB


def enc_kernel(ids, place, cap_hbm, enc_hbm, mine, theirs, cap, enc, sems):
    tiles, n = enc.shape[0], SIDE
    rows = cap.shape[0] // n
    loads = [pltpu.make_async_copy(enc_hbm.at[:, pl.ds(i * LB, LB)], enc.at[i], sems.at[i]) for i in range(tiles)]
    caps = [
        pltpu.make_async_copy(cap_hbm.at[pl.ds(i * rows, rows)], cap.at[pl.ds(i * rows, rows)], sems.at[tiles + i])
        for i in range(n)
    ]
    for copy in loads + caps:
        copy.start()
    for copy in loads:
        copy.wait()
    core, first, second = place[0], place[1], place[2]

    def body(b, carry):
        w = jnp.concatenate([enc[ids[core, b]], enc[ids[1 - core, b]]], axis=1)
        out = jnp.dot(cap[rows_of(b), :], w, preferred_element_type=F32).astype(BF)
        mine[rows_of(sent_at(b, first)), :] = out[:, :LB]
        theirs[rows_of(sent_at(b, second)), :] = out[:, LB:]
        return carry

    for i in range(n):
        caps[i].wait()
        lax.fori_loop(i * (NTB // n), (i + 1) * (NTB // n), body, 0, unroll=8)


def encode(ids, place, captured, enc):
    tiles = enc.shape[1] // LB
    return call(
        enc_kernel,
        "encode",
        [SMEM, SMEM, HBM, HBM],
        [shape(NTB * TB, LB)] * 2,
        (ids, place, captured, enc),
        MATMUL * enc.shape[0],
        [
            pltpu.VMEM(captured.shape, BF),
            pltpu.VMEM((tiles, enc.shape[0], LB), BF),
            pltpu.SemaphoreType.DMA((tiles + SIDE,)),
        ],
        limit=ENCODE_LIMIT,
    )


def split_add_kernel(mine, got, *quarters):
    for k in range(len(quarters)):
        quarters[k][...] = total((mine, got), slice(k * QB * TB, (k + 1) * QB * TB)).astype(BF)


def total4(refs, rows=slice(None)):
    return total(refs[:2], rows) + total(refs[2:4], rows)


def quarter_sum_kernel(*refs):
    out = total4(refs[:SIDE]).astype(BF)
    for ref in refs[-SIDE:]:
        ref[...] = out


SWAP = [(0, 1), (1, 0)]


def swap(x):
    return lax.ppermute(x, "core", SWAP)


def tok_perm(first, step):
    pairs = []
    for y in range(NY):
        for x in range(NX):
            for c in range(NC):
                ty, tx = (y, (x + step) % NX) if (c == 0) == first else ((y + step) % NY, x)
                pairs.append(((y * NX + x) * NC + c, (ty * NX + tx) * NC + c))
    return pairs


def send(x, first, step):
    return lax.ppermute(x, ("y", "x", "core"), tok_perm(first, step))


def copy_kernel(x, out):
    out[...] = x[...]


def tok_scatter(mine, theirs, beside=(), stage=False):
    got = [swap(t) for t in theirs]
    if stage:
        mine = [call(copy_kernel, "stage", [VMEM], shape(*mine[0].shape), mine, 0)]
    quarters = [
        q
        for m, g in zip(mine, got)
        for q in call(
            split_add_kernel, "split_add", [VMEM] * 2, [shape(QB * TB, LB)] * (SIDE // len(mine)), (m, g), m.size
        )
    ]
    terms = [quarters[3]] + [send(quarters[k - 1], True, k) for k in (2, 1, 3)]
    copies = call(
        quarter_sum_kernel,
        "quarter_sum",
        [VMEM] * (SIDE + len(beside)),
        [shape(QB * TB, LB)] * SIDE,
        (*terms, *beside),
        4 * quarters[0].size,
    )
    return [copies[0]] + [send(copies[k], False, k) for k in (2, 1, 3)]


def tok_gather(copies):
    got = {k: send(copies[k], True, k) for k in (2, 1, 3)}
    mine = [copies[0]] + [got[k] for k in range(1, SIDE)]
    return mine, [swap(q) for q in mine]


def join_slots(meta, mine, other, both):
    for k in range(SIDE):
        both[rows_of(ring4(meta[FIRST], -k) * QB, QB), :LB] = mine[k][...]
        both[rows_of(ring4(meta[SECOND], -k) * QB, QB), LB:] = other[k][...]


def codes_kernel(meta, *refs):
    terms, bias, copies = refs[:SIDE], refs[SIDE], refs[SIDE + 1 :]
    core = meta[CORE]
    for q in range(QB):
        block = meta[FIRST] * QB + q
        rows = slice(q * TB, (q + 1) * TB)
        v = total4(terms, rows) + bias[pl.ds(meta[KS * block + core], 1), :]
        soft = jnp.maximum(v, 0.0) + jnp.log1p(jnp.exp(-jnp.abs(v)))
        code = jnp.where(core < meta[COUNTS + block], soft, 0.0).astype(BF)
        for ref in copies:
            ref[rows, :] = code


def dpre_kernel(*refs):
    terms, own, copies = refs[:SIDE], refs[SIDE], refs[SIDE + 1 :]
    grads = (total4(terms) + PENALTY) * (1.0 - jnp.exp(-own[...].astype(F32)))
    for i in range(QB):
        tile = slice(i * TB, (i + 1) * TB)
        turned = grads[tile, :].T.astype(BF)
        for ref in copies:
            ref[tile, :] = turned


ORDER = (0, 1, 7, 2, 6, 3, 5, 4, 4)
NP = len(ORDER)


def piece_shapes(feats):
    return [shape(FULL, feats)] * 7 + [shape(HALF, feats)] * 2


def blocks_of(meta, pieces, slots=range(NP)):
    for slot in slots:
        chunk = lax.rem(meta[ZPOS] + ORDER[slot], NZ)
        for chain in range(CHAINS):
            ref = pieces[chain * NP + slot]
            base = chunk * ZB * CHAINS + chain * ZB + (ZB // 2 if slot == 8 else 0)
            for j in range(ref.shape[0] // TB):
                yield base + j, ref, slice(j * TB, (j + 1) * TB)


def dec_rows(meta, dec, block):
    ia, ib = pair_of(meta, block)
    return jnp.concatenate([dec[rows_of(ia), :], dec[rows_of(ib), :]], axis=0)


def parts_of(meta, dec, both, pieces, slots):
    for block, piece, rows in blocks_of(meta, pieces, slots):
        out = jnp.dot(both[rows_of(block), :], dec_rows(meta, dec, block), preferred_element_type=F32)
        piece[rows, :] = out.astype(BF)


def far_parts_kernel(meta, dec, *refs):
    both, pieces = refs[2 * SIDE], refs[2 * SIDE + 1 :]
    join_slots(meta, refs[:SIDE], refs[SIDE : 2 * SIDE], both)
    pieces = [None] * 7 + list(pieces[:2]) + [None] * 7 + list(pieces[2:])
    parts_of(meta, dec, both, pieces, (7, 8))


def near_parts_kernel(meta, dec, both, *pieces):
    pieces = list(pieces[:7]) + [None] * 2 + list(pieces[7:]) + [None] * 2
    parts_of(meta, dec, both, pieces, (5, 6, 3, 4, 1, 2, 0))


def make_parts(meta, mine, other, dec):
    feats = dec.shape[1]
    shapes = piece_shapes(feats)
    both, *far = call(
        far_parts_kernel,
        "far_parts",
        [SMEM] + [VMEM] * (1 + 2 * SIDE),
        [shape(NTB * TB, KS * LB)] + shapes[7:] * CHAINS,
        (meta, dec, *mine, *other),
        MATMUL * feats // 8,
    )
    near = call(
        near_parts_kernel,
        "near_parts",
        [SMEM] + [VMEM] * 2,
        shapes[:7] * CHAINS,
        (meta, dec, both),
        MATMUL * feats,
    )
    return both, [[*near[c * 7 : c * 7 + 7], *far[c * 2 : c * 2 + 2]] for c in range(CHAINS)]


def add_kernel(pa, ra, pb, rb, oa, ob):
    oa[...] = total((pa, ra)).astype(BF)
    ob[...] = total((pb, rb)).astype(BF)


def add_first_kernel(pa, ra, pb, rb, oa, ob):
    oa[:HALF, :] = (pa[:HALF, :].astype(F32) + ra[...].astype(F32)).astype(BF)
    oa[HALF:, :] = pa[HALF:, :]
    ob[:HALF, :] = pb[:HALF, :]
    ob[HALF:, :] = (pb[HALF:, :].astype(F32) + rb[...].astype(F32)).astype(BF)


def add_both(kernel, *args):
    return call(kernel, "ring_add", [VMEM] * 4, [shape(*args[0].shape)] * 2, args, args[0].size)


def delta_kernel(chain, meta, part, ra, rb, bias, cap, out):
    rows = rows_of((meta[ZPOS] * CHAINS + chain) * ZB, ZB)
    rec = total((part, ra, rb))
    out[...] = (SCALE_ERR * (rec + bias[...] - cap[rows, :].astype(F32))).astype(BF)


RIGHT = [(i, (i + 1) % NZ) for i in range(NZ)]
LEFT = [(i, (i - 1) % NZ) for i in range(NZ)]


def to_right(x):
    return lax.ppermute(x, "lat", RIGHT)


def to_left(x):
    return lax.ppermute(x, "lat", LEFT)


def reduce_z(meta, chains, bias, captured):
    moving = [(to_right(p[7]), to_left(p[8])) for p in chains]
    for slot in (5, 3, 1):
        kernel = add_first_kernel if slot == 5 else add_kernel
        sums = [add_both(kernel, p[slot], r, p[slot + 1], l) for p, (r, l) in zip(chains, moving)]
        moving = [(to_right(a), to_left(b)) for a, b in sums]
    return [
        call(
            functools.partial(delta_kernel, c),
            "delta",
            [SMEM] + [VMEM] * 5,
            shape(*p[0].shape),
            (meta, p[0], r, l, bias, captured),
            6 * p[0].size,
        )
        for c, (p, (r, l)) in enumerate(zip(chains, moving))
    ]


def gather_z(deltas):
    out = [[own] for own in deltas]
    moving = [(own, own) for own in deltas]
    for _ in range(3):
        moving = [(to_right(r), to_left(l)) for r, l in moving]
        for pieces, (r, l) in zip(out, moving):
            pieces += [l, r]
    for pieces, (r, l) in zip(out, moving):
        pieces += [to_right(r[:HALF]), to_left(l[HALF:])]
    return [piece for pieces in out for piece in pieces]


def dcodes_of(meta, dec, pieces, slots, put):
    for block, piece, rows in blocks_of(meta, pieces, slots):
        out = lax.dot_general(
            piece[rows, :], dec_rows(meta, dec, block), (((1,), (1,)), ((), ())), preferred_element_type=F32
        ).astype(BF)
        put(0, sent_at(block, meta[FIRST]), out[:, :LB])
        put(1, sent_at(block, meta[SECOND]), out[:, LB:])


def near_dcodes_kernel(meta, dec, *refs):
    pieces = list(refs[:7]) + [None] * 2 + list(refs[7:14]) + [None] * 2
    outs = refs[14:]

    def put(i, at, value):
        outs[i][rows_of(at), :] = value

    dcodes_of(meta, dec, pieces, range(7), put)


def all_dcodes_kernel(meta, dec, near_mine, near_theirs, *refs):
    outs = refs[-2:]
    outs[0][...] = near_mine[...]
    outs[1][...] = near_theirs[...]

    def put(i, at, value):
        outs[i][rows_of(at), :] = value

    pieces = [None] * 7 + list(refs[:2]) + [None] * 7 + list(refs[2:4])
    dcodes_of(meta, dec, pieces, (7, 8), put)


def make_dcodes(meta, dec, pieces):
    out = shape(NTB * TB, LB)
    near = [p for c in range(CHAINS) for p in pieces[c * NP : c * NP + 7]]
    far = [p for c in range(CHAINS) for p in pieces[c * NP + 7 : c * NP + 9]]
    flops = MATMUL * dec.shape[1]
    first = call(
        near_dcodes_kernel, "near_dcodes", [SMEM] + [VMEM] * (1 + len(near)), [out, out], (meta, dec, *near), flops
    )
    return call(
        all_dcodes_kernel,
        "all_dcodes",
        [SMEM] + [VMEM] * (3 + len(far)),
        [out, out],
        (meta, dec, *first, *far),
        flops // 8,
    )


def accumulate(meta, both, right, acc):
    def body(b, carry):
        ia, ib = pair_of(meta, b)
        prod = lax.dot_general(
            both[rows_of(b), :], right[rows_of(b), :], (((0,), (0,)), ((), ())), preferred_element_type=F32
        )
        acc[rows_of(ia), :] += prod[:LB]
        acc[rows_of(ib), :] += prod[LB:]
        return carry

    acc[...] = jnp.zeros_like(acc)
    lax.fori_loop(0, NTB, body, 0, unroll=4)


def dec_grad_kernel(meta, both, *refs):
    pieces, (out, done, delta, acc) = refs[:-4], refs[-4:]
    for block, piece, rows in blocks_of(meta, pieces):
        delta[rows_of(block), :] = piece[rows, :]
    accumulate(meta, both, delta, acc)
    out[...] = acc[...].astype(BF)
    done[...] = delta[: done.shape[0], : done.shape[1]]


def make_dec_grad(meta, like, both, pieces):
    return call(
        dec_grad_kernel,
        "dec_grad",
        [SMEM] + [VMEM] * (1 + len(pieces)),
        [shape(*like.shape), shape(16, LB)],
        (meta, both, *pieces),
        MATMUL * like.shape[1],
        [pltpu.VMEM((NTB * TB, like.shape[1]), BF), pltpu.VMEM(like.shape, F32)],
    )


def enc_grad_kernel(meta, cap, *refs):
    out, both, acc = refs[2 * SIDE :]
    for slot, (quarters, at) in enumerate(((refs[:SIDE], FIRST), (refs[SIDE : 2 * SIDE], SECOND))):
        for k in range(SIDE):
            for i in range(QB):
                row = ((ring4(meta[at], -k) * QB + i) * KS + slot)
                both[rows_of(row), :] = quarters[k][i * LB : (i + 1) * LB, :]

    def body(b, carry):
        ia, ib = pair_of(meta, b)
        prod = jnp.dot(both[rows_of(b * KS, KS), :], cap[rows_of(b), :], preferred_element_type=F32)
        acc[rows_of(ia), :] += prod[:LB]
        acc[rows_of(ib), :] += prod[LB:]
        return carry

    acc[...] = jnp.zeros_like(acc)
    lax.fori_loop(0, NTB, body, 0, unroll=8)
    for i in range(acc.shape[0] // LB):
        tile = slice(i * LB, (i + 1) * LB)
        out[:, tile] = acc[tile, :].T.astype(BF)


def make_enc_grad(meta, captured, like, mine, other):
    return call(
        enc_grad_kernel,
        "enc_grad",
        [SMEM] + [VMEM] * (1 + 2 * SIDE),
        shape(*like.shape),
        (meta, captured, *mine, *other),
        MATMUL * like.shape[0],
        [pltpu.VMEM((NTB * KS * LB, TB), BF), pltpu.VMEM(like.shape[::-1], F32)],
    )


def local(captured, enc_weight, enc_bias, dec_weight, dec_bias, block_ids, block_counts):
    y, x, core = (lax.axis_index(a) for a in ("y", "x", "core"))
    first, second = jnp.where(core == 0, x, y), jnp.where(core == 0, y, x)
    place = jnp.stack([core, first, second, lax.axis_index("lat")]).astype(jnp.int32)
    meta = jnp.concatenate([block_ids.reshape(-1), block_counts.reshape(-1), place])

    sums = encode(block_ids.transpose(1, 2, 0).reshape(KS, -1), place, captured, enc_weight)
    terms = tok_scatter(sums[:1], sums[1:], stage=True)
    codes = call(
        codes_kernel,
        "codes",
        [SMEM] + [VMEM] * (SIDE + 1),
        [shape(*terms[0].shape)] * SIDE,
        (meta, *terms, enc_bias.reshape(-1, LB)),
        20 * terms[0].size,
    )
    both, chains = make_parts(meta, *tok_gather(codes), dec_weight)
    pieces = gather_z(reduce_z(meta, chains, dec_bias.reshape(1, -1), captured))
    dec_grad, done = make_dec_grad(meta, dec_weight, both, pieces)
    sums = make_dcodes(meta, dec_weight, pieces)
    terms = tok_scatter(sums[:1], sums[1:], beside=(done,))
    dpre = call(
        dpre_kernel,
        "dpre",
        [VMEM] * (SIDE + 1),
        [shape(*codes[0].shape)] * SIDE,
        (*terms, codes[0]),
        20 * codes[0].size,
    )
    enc_grad = make_enc_grad(meta, captured, enc_weight, *tok_gather(dpre))
    return enc_grad, dec_grad


def solution(mesh):
    cube = Mesh(mesh.devices.reshape(NY, NX, NC, NZ), ("y", "x", "core", "lat"))
    tok = ("y", "x", "core")
    in_specs = (
        P(None, tok),
        P(tok, "lat"),
        P("lat"),
        P("lat", tok),
        P(tok),
        P(None, "lat", None),
        P(None, "lat"),
    )
    out_specs = (P(tok, "lat"), P("lat", tok))
    return jax.shard_map(local, mesh=cube, in_specs=in_specs, out_specs=out_specs, check_vma=False)
```

```python
import functools

import jax
import jax.numpy as jnp
from jax import lax
from jax.experimental import pallas as pl
from jax.experimental.pallas import tpu as pltpu
from jax.sharding import Mesh, PartitionSpec as P

TB = 128
LB = 128
KS = 2
NTB = 32
NY, NX, NC, NZ = 4, 4, 2, 8
SIDE = 4
CHAINS = 2
QB = NTB // SIDE
ZB = NTB // NZ // CHAINS
FULL = ZB * TB
HALF = FULL // 2

SCALE_ERR = 0.0625
PENALTY = 0.05

BF = jnp.bfloat16
F32 = jnp.float32
VMEM_LIMIT = 24 * 1024 * 1024
ENCODE_LIMIT = 60 * 1024 * 1024

COUNTS = NTB * KS
CORE, FIRST, SECOND, ZPOS = (COUNTS + NTB + i for i in range(4))

SMEM = pl.BlockSpec(memory_space=pltpu.SMEM)
VMEM = pl.BlockSpec(memory_space=pltpu.VMEM)
HBM = pl.BlockSpec(memory_space=pltpu.HBM)


def cost(flops, nbytes):
    return pl.CostEstimate(flops=flops, bytes_accessed=nbytes, transcendentals=0)


def call(kernel, name, in_specs, out_shape, args, flops, scratch=(), aliases=None, limit=VMEM_LIMIT):
    outs = out_shape if isinstance(out_shape, list) else [out_shape]
    nbytes = sum(a.size * a.dtype.itemsize for a in (*args, *outs))
    return pl.pallas_call(
        kernel,
        in_specs=in_specs,
        out_specs=[VMEM] * len(out_shape) if isinstance(out_shape, list) else VMEM,
        out_shape=out_shape,
        scratch_shapes=list(scratch),
        input_output_aliases=aliases or {},
        compiler_params=pltpu.CompilerParams(vmem_limit_bytes=limit),
        cost_estimate=cost(flops, nbytes),
        name=name,
    )(*args)


def shape(*dims, dtype=BF):
    return jax.ShapeDtypeStruct(dims, dtype)


def rows_of(block, count=1):
    return pl.ds(pl.multiple_of(block * TB, TB), count * TB)


def pair_of(meta, block):
    core = meta[CORE]
    return meta[KS * block + core], meta[KS * block + 1 - core]


def ring4(place, step):
    return lax.rem(place + step + SIDE, SIDE)


def sent_at(block, place):
    return lax.rem(block // QB + 2 * SIDE - 1 - place, SIDE) * QB + lax.rem(block, QB)


def total(refs, rows=slice(None)):
    out = refs[0][rows, :].astype(F32)
    for ref in refs[1:]:
        out += ref[rows, :].astype(F32)
    return out


MATMUL = 2 * NTB * TB * KS * LB


def enc_kernel(ids, place, cap_hbm, enc_hbm, mine, theirs, cap, enc, sems):
    tiles, n = enc.shape[0], SIDE
    rows = cap.shape[0] // n
    loads = [pltpu.make_async_copy(enc_hbm.at[:, pl.ds(i * LB, LB)], enc.at[i], sems.at[i]) for i in range(tiles)]
    caps = [
        pltpu.make_async_copy(cap_hbm.at[pl.ds(i * rows, rows)], cap.at[pl.ds(i * rows, rows)], sems.at[tiles + i])
        for i in range(n)
    ]
    for copy in loads + caps:
        copy.start()
    for copy in loads:
        copy.wait()
    core, first, second = place[0], place[1], place[2]

    def body(b, carry):
        w = jnp.concatenate([enc[ids[core, b]], enc[ids[1 - core, b]]], axis=1)
        out = jnp.dot(cap[rows_of(b), :], w, preferred_element_type=F32).astype(BF)
        mine[rows_of(sent_at(b, first)), :] = out[:, :LB]
        theirs[rows_of(sent_at(b, second)), :] = out[:, LB:]
        return carry

    for i in range(n):
        caps[i].wait()
        lax.fori_loop(i * (NTB // n), (i + 1) * (NTB // n), body, 0, unroll=8)


def encode(ids, place, captured, enc):
    tiles = enc.shape[1] // LB
    return call(
        enc_kernel,
        "encode",
        [SMEM, SMEM, HBM, HBM],
        [shape(NTB * TB, LB)] * 2,
        (ids, place, captured, enc),
        MATMUL * enc.shape[0],
        [
            pltpu.VMEM(captured.shape, BF),
            pltpu.VMEM((tiles, enc.shape[0], LB), BF),
            pltpu.SemaphoreType.DMA((tiles + SIDE,)),
        ],
        limit=ENCODE_LIMIT,
    )


def split_add_kernel(mine, got, *quarters):
    for k in range(len(quarters)):
        quarters[k][...] = total((mine, got), slice(k * QB * TB, (k + 1) * QB * TB)).astype(BF)


def total4(refs, rows=slice(None)):
    return total(refs[:2], rows) + total(refs[2:4], rows)


def quarter_sum_kernel(*refs):
    out = total4(refs[:SIDE]).astype(BF)
    for ref in refs[-SIDE:]:
        ref[...] = out


SWAP = [(0, 1), (1, 0)]


def swap(x):
    return lax.ppermute(x, "core", SWAP)


def tok_perm(first, step):
    pairs = []
    for y in range(NY):
        for x in range(NX):
            for c in range(NC):
                ty, tx = (y, (x + step) % NX) if (c == 0) == first else ((y + step) % NY, x)
                pairs.append(((y * NX + x) * NC + c, (ty * NX + tx) * NC + c))
    return pairs


def send(x, first, step):
    return lax.ppermute(x, ("y", "x", "core"), tok_perm(first, step))


def copy_kernel(x, out):
    out[...] = x[...]


def tok_scatter(mine, theirs, beside=(), stage=False):
    got = [swap(t) for t in theirs]
    if stage:
        mine = [call(copy_kernel, "stage", [VMEM], shape(*mine[0].shape), mine, 0)]
    quarters = [
        q
        for m, g in zip(mine, got)
        for q in call(
            split_add_kernel, "split_add", [VMEM] * 2, [shape(QB * TB, LB)] * (SIDE // len(mine)), (m, g), m.size
        )
    ]
    terms = [quarters[3]] + [send(quarters[k - 1], True, k) for k in (2, 1, 3)]
    copies = call(
        quarter_sum_kernel,
        "quarter_sum",
        [VMEM] * (SIDE + len(beside)),
        [shape(QB * TB, LB)] * SIDE,
        (*terms, *beside),
        4 * quarters[0].size,
    )
    return [copies[0]] + [send(copies[k], False, k) for k in (2, 1, 3)]


def tok_gather(copies):
    got = {k: send(copies[k], True, k) for k in (2, 1, 3)}
    mine = [copies[0]] + [got[k] for k in range(1, SIDE)]
    return mine, [swap(q) for q in mine]


def join_slots(meta, mine, other, both):
    for k in range(SIDE):
        both[rows_of(ring4(meta[FIRST], -k) * QB, QB), :LB] = mine[k][...]
        both[rows_of(ring4(meta[SECOND], -k) * QB, QB), LB:] = other[k][...]


def codes_kernel(meta, *refs):
    terms, bias, copies = refs[:SIDE], refs[SIDE], refs[SIDE + 1 :]
    core = meta[CORE]
    for q in range(QB):
        block = meta[FIRST] * QB + q
        rows = slice(q * TB, (q + 1) * TB)
        v = total4(terms, rows) + bias[pl.ds(meta[KS * block + core], 1), :]
        soft = jnp.maximum(v, 0.0) + jnp.log1p(jnp.exp(-jnp.abs(v)))
        code = jnp.where(core < meta[COUNTS + block], soft, 0.0).astype(BF)
        for ref in copies:
            ref[rows, :] = code


def dpre_kernel(*refs):
    terms, own, copies = refs[:SIDE], refs[SIDE], refs[SIDE + 1 :]
    grads = (total4(terms) + PENALTY) * (1.0 - jnp.exp(-own[...].astype(F32)))
    for i in range(QB):
        tile = slice(i * TB, (i + 1) * TB)
        turned = grads[tile, :].T.astype(BF)
        for ref in copies:
            ref[tile, :] = turned


ORDER = (0, 1, 7, 2, 6, 3, 5, 4, 4)
NP = len(ORDER)


def piece_shapes(feats):
    return [shape(FULL, feats)] * 7 + [shape(HALF, feats)] * 2


def blocks_of(meta, pieces, slots=range(NP)):
    for slot in slots:
        chunk = lax.rem(meta[ZPOS] + ORDER[slot], NZ)
        for chain in range(CHAINS):
            ref = pieces[chain * NP + slot]
            base = chunk * ZB * CHAINS + chain * ZB + (ZB // 2 if slot == 8 else 0)
            for j in range(ref.shape[0] // TB):
                yield base + j, ref, slice(j * TB, (j + 1) * TB)


def dec_rows(meta, dec, block):
    ia, ib = pair_of(meta, block)
    return jnp.concatenate([dec[rows_of(ia), :], dec[rows_of(ib), :]], axis=0)


def parts_of(meta, dec, both, pieces, slots):
    for block, piece, rows in blocks_of(meta, pieces, slots):
        out = jnp.dot(both[rows_of(block), :], dec_rows(meta, dec, block), preferred_element_type=F32)
        piece[rows, :] = out.astype(BF)


def far_parts_kernel(meta, dec, *refs):
    both, pieces = refs[2 * SIDE], refs[2 * SIDE + 1 :]
    join_slots(meta, refs[:SIDE], refs[SIDE : 2 * SIDE], both)
    pieces = [None] * 7 + list(pieces[:2]) + [None] * 7 + list(pieces[2:])
    parts_of(meta, dec, both, pieces, (7, 8))


def near_parts_kernel(meta, dec, both, *pieces):
    pieces = list(pieces[:7]) + [None] * 2 + list(pieces[7:]) + [None] * 2
    parts_of(meta, dec, both, pieces, (5, 6, 3, 4, 1, 2, 0))


def make_parts(meta, mine, other, dec):
    feats = dec.shape[1]
    shapes = piece_shapes(feats)
    both, *far = call(
        far_parts_kernel,
        "far_parts",
        [SMEM] + [VMEM] * (1 + 2 * SIDE),
        [shape(NTB * TB, KS * LB)] + shapes[7:] * CHAINS,
        (meta, dec, *mine, *other),
        MATMUL * feats // 8,
    )
    near = call(
        near_parts_kernel,
        "near_parts",
        [SMEM] + [VMEM] * 2,
        shapes[:7] * CHAINS,
        (meta, dec, both),
        MATMUL * feats,
    )
    return both, [[*near[c * 7 : c * 7 + 7], *far[c * 2 : c * 2 + 2]] for c in range(CHAINS)]


def add_kernel(pa, ra, pb, rb, oa, ob):
    oa[...] = total((pa, ra)).astype(BF)
    ob[...] = total((pb, rb)).astype(BF)


def add_first_kernel(pa, ra, pb, rb, oa, ob):
    oa[:HALF, :] = (pa[:HALF, :].astype(F32) + ra[...].astype(F32)).astype(BF)
    oa[HALF:, :] = pa[HALF:, :]
    ob[:HALF, :] = pb[:HALF, :]
    ob[HALF:, :] = (pb[HALF:, :].astype(F32) + rb[...].astype(F32)).astype(BF)


def add_both(kernel, *args):
    return call(kernel, "ring_add", [VMEM] * 4, [shape(*args[0].shape)] * 2, args, args[0].size)


def delta_kernel(chain, meta, part, ra, rb, bias, cap, out):
    rows = rows_of((meta[ZPOS] * CHAINS + chain) * ZB, ZB)
    rec = total((part, ra, rb))
    out[...] = (SCALE_ERR * (rec + bias[...] - cap[rows, :].astype(F32))).astype(BF)


RIGHT = [(i, (i + 1) % NZ) for i in range(NZ)]
LEFT = [(i, (i - 1) % NZ) for i in range(NZ)]


def to_right(x):
    return lax.ppermute(x, "lat", RIGHT)


def to_left(x):
    return lax.ppermute(x, "lat", LEFT)


def reduce_z(meta, chains, bias, captured):
    moving = [(to_right(p[7]), to_left(p[8])) for p in chains]
    for slot in (5, 3, 1):
        kernel = add_first_kernel if slot == 5 else add_kernel
        sums = [add_both(kernel, p[slot], r, p[slot + 1], l) for p, (r, l) in zip(chains, moving)]
        moving = [(to_right(a), to_left(b)) for a, b in sums]
    return [
        call(
            functools.partial(delta_kernel, c),
            "delta",
            [SMEM] + [VMEM] * 5,
            shape(*p[0].shape),
            (meta, p[0], r, l, bias, captured),
            6 * p[0].size,
        )
        for c, (p, (r, l)) in enumerate(zip(chains, moving))
    ]


def gather_z(deltas):
    out = [[own] for own in deltas]
    moving = [(own, own) for own in deltas]
    for _ in range(3):
        moving = [(to_right(r), to_left(l)) for r, l in moving]
        for pieces, (r, l) in zip(out, moving):
            pieces += [l, r]
    for pieces, (r, l) in zip(out, moving):
        pieces += [to_right(r[:HALF]), to_left(l[HALF:])]
    return [piece for pieces in out for piece in pieces]


def dcodes_of(meta, dec, pieces, slots, put):
    for block, piece, rows in blocks_of(meta, pieces, slots):
        out = lax.dot_general(
            piece[rows, :], dec_rows(meta, dec, block), (((1,), (1,)), ((), ())), preferred_element_type=F32
        ).astype(BF)
        put(0, sent_at(block, meta[FIRST]), out[:, :LB])
        put(1, sent_at(block, meta[SECOND]), out[:, LB:])


def near_dcodes_kernel(meta, dec, *refs):
    pieces = list(refs[:7]) + [None] * 2 + list(refs[7:14]) + [None] * 2
    outs = refs[14:]

    def put(i, at, value):
        outs[i][rows_of(at), :] = value

    dcodes_of(meta, dec, pieces, range(7), put)


def all_dcodes_kernel(meta, dec, near_mine, near_theirs, *refs):
    outs = refs[-2:]
    outs[0][...] = near_mine[...]
    outs[1][...] = near_theirs[...]

    def put(i, at, value):
        outs[i][rows_of(at), :] = value

    pieces = [None] * 7 + list(refs[:2]) + [None] * 7 + list(refs[2:4])
    dcodes_of(meta, dec, pieces, (7, 8), put)


def make_dcodes(meta, dec, pieces):
    out = shape(NTB * TB, LB)
    near = [p for c in range(CHAINS) for p in pieces[c * NP : c * NP + 7]]
    far = [p for c in range(CHAINS) for p in pieces[c * NP + 7 : c * NP + 9]]
    flops = MATMUL * dec.shape[1]
    first = call(
        near_dcodes_kernel, "near_dcodes", [SMEM] + [VMEM] * (1 + len(near)), [out, out], (meta, dec, *near), flops
    )
    return call(
        all_dcodes_kernel,
        "all_dcodes",
        [SMEM] + [VMEM] * (3 + len(far)),
        [out, out],
        (meta, dec, *first, *far),
        flops // 8,
    )


def accumulate(meta, both, right, acc):
    def body(b, carry):
        ia, ib = pair_of(meta, b)
        prod = lax.dot_general(
            both[rows_of(b), :], right[rows_of(b), :], (((0,), (0,)), ((), ())), preferred_element_type=F32
        )
        acc[rows_of(ia), :] += prod[:LB]
        acc[rows_of(ib), :] += prod[LB:]
        return carry

    acc[...] = jnp.zeros_like(acc)
    lax.fori_loop(0, NTB, body, 0, unroll=8)


def dec_grad_kernel(meta, both, *refs):
    pieces, (out, done, delta, acc) = refs[:-4], refs[-4:]
    for block, piece, rows in blocks_of(meta, pieces):
        delta[rows_of(block), :] = piece[rows, :]
    accumulate(meta, both, delta, acc)
    out[...] = acc[...].astype(BF)
    done[...] = delta[: done.shape[0], : done.shape[1]]


def make_dec_grad(meta, like, both, pieces):
    return call(
        dec_grad_kernel,
        "dec_grad",
        [SMEM] + [VMEM] * (1 + len(pieces)),
        [shape(*like.shape), shape(16, LB)],
        (meta, both, *pieces),
        MATMUL * like.shape[1],
        [pltpu.VMEM((NTB * TB, like.shape[1]), BF), pltpu.VMEM(like.shape, F32)],
    )


def enc_grad_kernel(meta, cap, *refs):
    out, both, acc = refs[2 * SIDE :]
    for slot, (quarters, at) in enumerate(((refs[:SIDE], FIRST), (refs[SIDE : 2 * SIDE], SECOND))):
        for k in range(SIDE):
            for i in range(QB):
                row = ((ring4(meta[at], -k) * QB + i) * KS + slot)
                both[rows_of(row), :] = quarters[k][i * LB : (i + 1) * LB, :]

    def body(b, carry):
        ia, ib = pair_of(meta, b)
        prod = jnp.dot(both[rows_of(b * KS, KS), :], cap[rows_of(b), :], preferred_element_type=F32)
        acc[rows_of(ia), :] += prod[:LB]
        acc[rows_of(ib), :] += prod[LB:]
        return carry

    acc[...] = jnp.zeros_like(acc)
    lax.fori_loop(0, NTB, body, 0, unroll=8)
    for i in range(acc.shape[0] // LB):
        tile = slice(i * LB, (i + 1) * LB)
        out[:, tile] = acc[tile, :].T.astype(BF)


def make_enc_grad(meta, captured, like, mine, other):
    return call(
        enc_grad_kernel,
        "enc_grad",
        [SMEM] + [VMEM] * (1 + 2 * SIDE),
        shape(*like.shape),
        (meta, captured, *mine, *other),
        MATMUL * like.shape[0],
        [pltpu.VMEM((NTB * KS * LB, TB), BF), pltpu.VMEM(like.shape[::-1], F32)],
    )


def local(captured, enc_weight, enc_bias, dec_weight, dec_bias, block_ids, block_counts):
    y, x, core = (lax.axis_index(a) for a in ("y", "x", "core"))
    first, second = jnp.where(core == 0, x, y), jnp.where(core == 0, y, x)
    place = jnp.stack([core, first, second, lax.axis_index("lat")]).astype(jnp.int32)
    meta = jnp.concatenate([block_ids.reshape(-1), block_counts.reshape(-1), place])

    sums = encode(block_ids.transpose(1, 2, 0).reshape(KS, -1), place, captured, enc_weight)
    terms = tok_scatter(sums[:1], sums[1:], stage=True)
    codes = call(
        codes_kernel,
        "codes",
        [SMEM] + [VMEM] * (SIDE + 1),
        [shape(*terms[0].shape)] * SIDE,
        (meta, *terms, enc_bias.reshape(-1, LB)),
        20 * terms[0].size,
    )
    both, chains = make_parts(meta, *tok_gather(codes), dec_weight)
    pieces = gather_z(reduce_z(meta, chains, dec_bias.reshape(1, -1), captured))
    dec_grad, done = make_dec_grad(meta, dec_weight, both, pieces)
    sums = make_dcodes(meta, dec_weight, pieces)
    terms = tok_scatter(sums[:1], sums[1:], beside=(done,))
    dpre = call(
        dpre_kernel,
        "dpre",
        [VMEM] * (SIDE + 1),
        [shape(*codes[0].shape)] * SIDE,
        (*terms, codes[0]),
        20 * codes[0].size,
    )
    enc_grad = make_enc_grad(meta, captured, enc_weight, *tok_gather(dpre))
    return enc_grad, dec_grad


def solution(mesh):
    cube = Mesh(mesh.devices.reshape(NY, NX, NC, NZ), ("y", "x", "core", "lat"))
    tok = ("y", "x", "core")
    in_specs = (
        P(None, tok),
        P(tok, "lat"),
        P("lat"),
        P("lat", tok),
        P(tok),
        P(None, "lat", None),
        P(None, "lat"),
    )
    out_specs = (P(tok, "lat"), P("lat", tok))
    return jax.shard_map(local, mesh=cube, in_specs=in_specs, out_specs=out_specs, check_vma=False)
```
